256 devices in a mesh: frame: 32 (over z, x_hi, core), chan: 8 (over y, x_lo).
Axes of the slice: x: 4 (x_hi: 2, x_lo: 2; x = x_hi * 2 + x_lo), y: 4, z: 8, core: 2. Of those that a mesh axis runs over, the one named last changes fastest.
Arguments:
- inputs: bfloat16 [32, 128, 32, 1024], P('frame', None, None, 'chan'), may hold values from -6 to 6
- cotangent: bfloat16 [32, 128, 32, 1024], P('frame', None, None, 'chan'), may hold values from -6 to 6
- spatial_weight: bfloat16 [9, 128, 128], replicated, may hold values from -0.1875 to 0.1875
- temporal_weight: bfloat16 [3, 128, 128], replicated, may hold values from -0.3125 to 0.3125
- norm_gain: float32 [128], replicated, may hold values from 0.1 to 1.9
- norm_shift: float32 [128], replicated, may hold values from -3 to 3
- spatial_bias: float32 [128], replicated, may hold values from -3 to 3
Outputs:
- output: bfloat16 [32, 128, 32, 1024], P('frame', None, None, 'chan')
- input_grad: bfloat16 [32, 128, 32, 1024], P('frame', None, None, 'chan')
- spatial_grad: float32 [9, 128, 128], replicated
- temporal_grad: float32 [3, 128, 128], replicated
The draws below stay inside these ranges and needn't reach their ends.
All inputs are finite; a program needn't handle non-finite values.
Results may differ from the reference program's by a relative error of at most 0.00105.
The reference program's roundings to bfloat16 on the way (of `active`, `hidden` and `grad_pre`) count: a program that leaves them out, or rounds other values in their place, can miss the bound.
Values may be sent and summed in bfloat16 or wider, within the bound.
No kernel may reach another device: no remote copies, remote signals or barrier semaphores. Data moves between devices by JAX's collectives and lax.ppermute only.
A program may use at most 128 MiB of HBM per device.

```python
import jax
import jax.numpy as jnp
from jax import lax

C = 128
GROUPS = 32
IMG_W = 1024
ROWS = 32
FRAMES = 32


def level_of(own_key, shape, shards, least, top_value):
    level = 1.0
    for axis_at, parts in shards:
        steps = jax.random.uniform(jax.random.fold_in(jax.random.fold_in(own_key, 6), axis_at), (parts,), jnp.float32, least / len(shards), top_value / len(shards))
        level = level * jnp.repeat(jnp.exp(steps), shape[axis_at] // parts).reshape((-1,) + (1,) * (len(shape) - 1 - axis_at))
    return level


def noise(own_key, shape, scale, limit, cuts=(), kind=jnp.bfloat16):
    result = jax.random.normal(own_key, shape, jnp.float32) * scale
    if len(cuts) > 0:
        result = level_of(own_key, shape, cuts, -0.22, 0.18) * result
    return jnp.clip(result, min=-limit, max=limit).astype(kind)


def setup_inputs(seed: int = 0) -> dict:
    arg_keys = jax.random.split(jax.random.key(seed), 8)
    return {
        "inputs": noise(arg_keys[0], (FRAMES, C, ROWS, IMG_W), 1.0, 6.0, ((0, 32), (3, 8))),
        "cotangent": noise(arg_keys[1], (FRAMES, C, ROWS, IMG_W), 1.0, 6.0, ((0, 32), (3, 8))),
        "spatial_weight": noise(arg_keys[2], (9, C, C), (9 * C) ** -0.5, 0.1875),
        "temporal_weight": noise(arg_keys[3], (3, C, C), (3 * C) ** -0.5, 0.3125),
        "norm_gain": jnp.clip(1.0 + 0.18 * jax.random.normal(arg_keys[4], (C,), jnp.float32), 0.1, 1.9),
        "norm_shift": noise(arg_keys[5], (C,), 0.5, 3.0, (), jnp.float32),
        "spatial_bias": noise(arg_keys[6], (C,), 0.5, 3.0, (), jnp.float32),
    }


CONTRACT_FIRST = (((0,), (0,)), ((), ()))
CONTRACT_LAST = (((1,), (1,)), ((), ()))

def normalize(plane_in, norm_gain, norm_shift):
    channels = plane_in.shape[0]
    group_size = C // GROUPS
    grouped = plane_in.reshape(channels // group_size, -1)
    center = lax.optimization_barrier(jnp.mean(grouped, axis=1, keepdims=True))
    spread = lax.optimization_barrier(jnp.mean(jnp.square(grouped - center), axis=1, keepdims=True))
    inv_spread = lax.rsqrt(spread + 1e-05)
    normed = ((grouped - center) * inv_spread).reshape(plane_in.shape)
    shaped = normed * norm_gain[:, None, None] + norm_shift[:, None, None]
    return (normed, inv_spread, shaped)

def group_back(grad_field, normed, inv_spread, norm_gain):
    channels = grad_field.shape[0]
    group_size = C // GROUPS
    scaled = (grad_field * norm_gain[:, None, None]).reshape(channels // group_size, -1)
    flat_normed = normed.reshape(channels // group_size, -1)
    mean_grad = lax.optimization_barrier(jnp.mean(scaled, axis=1, keepdims=True))
    second = lax.optimization_barrier(jnp.mean(scaled * flat_normed, axis=1, keepdims=True))
    return (inv_spread * (scaled - mean_grad - flat_normed * second)).reshape(grad_field.shape)

def silu_slope(value):
    logistic = jax.nn.sigmoid(value)
    return logistic * (1.0 + value * (1.0 - logistic))

def shifted_tap(padded, stencil, band_rows, band_cols, mirrored):
    row_shift = stencil // 3
    col_shift = stencil % 3
    if mirrored:
        row_shift = 2 - row_shift
        col_shift = 2 - col_shift
    window_part = padded[:, row_shift:row_shift + band_rows, col_shift:col_shift + band_cols]
    return window_part.reshape(window_part.shape[0], band_rows * band_cols)

def reference(inputs, cotangent, spatial_weight, temporal_weight, norm_gain, norm_shift, spatial_bias):
    frames = inputs.shape[0]
    band_rows = inputs.shape[2]
    band_cols = inputs.shape[3]
    pixels = band_rows * band_cols

    def spatial_conv(active):
        padded = jnp.pad(active, ((0, 0), (1, 1), (1, 1)))
        summed = jnp.zeros((C, pixels), jnp.float32)
        for stencil in range(9):
            summed = summed + jnp.dot(spatial_weight[stencil], shifted_tap(padded, stencil, band_rows, band_cols, False), preferred_element_type=jnp.float32)
        return summed + spatial_bias[:, None]

    def forward_frame(frame_in):
        normed, inv_spread, shaped = normalize(frame_in.astype(jnp.float32), norm_gain, norm_shift)
        active = jax.nn.silu(shaped).astype(jnp.bfloat16)
        return jax.nn.silu(spatial_conv(active)).astype(jnp.bfloat16)
    hidden = lax.map(forward_frame, inputs)
    hidden_pad = jnp.pad(hidden, ((1, 1), (0, 0), (0, 0)))
    grad_all = cotangent.reshape(frames, C, pixels)
    grad_pad = jnp.pad(grad_all, ((1, 1), (0, 0), (0, 0)))

    def frame_step(state_in, index):
        spatial_acc, temporal_acc = state_in
        frame_in = lax.dynamic_index_in_dim(inputs, index, 0, keepdims=False)
        grad_out = lax.dynamic_index_in_dim(grad_all, index, 0, keepdims=False)
        hidden_win = lax.dynamic_slice_in_dim(hidden_pad, index, 3, 0)
        grad_win = lax.dynamic_slice_in_dim(grad_pad, index, 3, 0)
        mixed = jnp.zeros((C, pixels), jnp.float32)
        back_grad = jnp.zeros((C, pixels), jnp.float32)
        for k in range(3):
            mixed = mixed + jnp.dot(temporal_weight[k], hidden_win[k], preferred_element_type=jnp.float32)
            back_grad = back_grad + lax.dot_general(temporal_weight[k], grad_win[2 - k], CONTRACT_FIRST, preferred_element_type=jnp.float32)
        temporal_acc = temporal_acc + jnp.stack([lax.dot_general(grad_out, hidden_win[k], CONTRACT_LAST, preferred_element_type=jnp.float32) for k in range(3)])
        plane_in = frame_in.astype(jnp.float32)
        output = (plane_in.reshape(C, pixels) + mixed).astype(jnp.bfloat16)
        normed, inv_spread, shaped = normalize(plane_in, norm_gain, norm_shift)
        active = jax.nn.silu(shaped).astype(jnp.bfloat16)
        preact = spatial_conv(active)
        grad_pre = (back_grad * silu_slope(preact)).astype(jnp.bfloat16)
        grad_padded = jnp.pad(grad_pre.reshape(C, band_rows, band_cols), ((0, 0), (1, 1), (1, 1)))
        act_padded = jnp.pad(active, ((0, 0), (1, 1), (1, 1)))
        input_part = jnp.zeros((C, pixels), jnp.float32)
        weight_terms = []
        for stencil in range(9):
            input_part = input_part + lax.dot_general(spatial_weight[stencil], shifted_tap(grad_padded, stencil, band_rows, band_cols, True), CONTRACT_FIRST, preferred_element_type=jnp.float32)
            weight_terms.append(lax.dot_general(grad_pre, shifted_tap(act_padded, stencil, band_rows, band_cols, False), CONTRACT_LAST, preferred_element_type=jnp.float32))
        spatial_acc = spatial_acc + jnp.stack(weight_terms)
        grad_field = input_part.reshape(C, band_rows, band_cols) * silu_slope(shaped)
        input_grad = (grad_out.astype(jnp.float32).reshape(C, band_rows, band_cols) + group_back(grad_field, normed, inv_spread, norm_gain)).astype(jnp.bfloat16)
        return ((spatial_acc, temporal_acc), (output.reshape(C, band_rows, band_cols), input_grad))
    start_state = (jnp.zeros((9, C, C), jnp.float32), jnp.zeros((3, C, C), jnp.float32))
    totals, stacked = lax.scan(frame_step, start_state, jnp.arange(frames, dtype=jnp.int32))
    return (stacked[0], stacked[1], totals[0], totals[1])
```

```python
import jax
import jax.numpy as jnp
from jax import lax
from jax.sharding import PartitionSpec as P

GROUPS = 32
CONTRACT_FIRST = (((0,), (0,)), ((), ()))
CONTRACT_LAST = (((1,), (1,)), ((), ()))


def silu_slope(value):
    logistic = jax.nn.sigmoid(value)
    return logistic * (1.0 + value * (1.0 - logistic))


def partner(bits, frames):
    return [(f, f ^ bits) for f in range(frames)]


def neighbour(frames):
    pairs = []
    for f in range(frames):
        target = f + 1 if f % 2 else f - 1
        if 0 <= target < frames:
            pairs.append((f, target))
    return pairs


def tap(padded, stencil, rows, cols, mirrored):
    dy, dx = stencil // 3, stencil % 3
    if mirrored:
        dy, dx = 2 - dy, 2 - dx
    part = padded[:, dy : dy + rows, dx : dx + cols]
    return part.reshape(part.shape[0], rows * cols)


def edges_to_peers(left, right, me, peers):
    below = lax.broadcasted_iota(jnp.int32, (peers, 1, 1), 0) < me
    return jnp.where(below, left[None], right[None])


def padded_plane(plane, low, high):
    return jnp.pad(
        jnp.concatenate([low[:, :, None], plane, high[:, :, None]], axis=2),
        ((0, 0), (1, 1), (0, 0)),
    )


def edge_of(received, me, peers, step):
    at = me + step
    found = lax.dynamic_index_in_dim(received, jnp.clip(at, 0, peers - 1), 0, keepdims=False)
    return jnp.where((at >= 0) & (at < peers), found, 0.0)


def body(inputs, cotangent, spatial_weight, temporal_weight, norm_gain, norm_shift, spatial_bias):
    frames = lax.axis_size("frame")
    peers = lax.axis_size("chan")
    me = lax.axis_index("chan")
    core = lax.axis_index("frame") % 2
    channels, rows, cols = inputs.shape[1:]
    pixels = rows * cols
    count = (channels // GROUPS) * pixels * peers

    grad_out = cotangent[0].reshape(channels, pixels)
    grad_cross = lax.ppermute(grad_out, "frame", neighbour(frames))
    grad_mate = lax.ppermute(grad_out, "frame", partner(1, frames))

    plane_in = inputs[0].astype(jnp.float32)
    own_mean = jnp.mean(plane_in, axis=(1, 2))
    own_square = jnp.sum(jnp.square(plane_in - own_mean[:, None, None]), axis=(1, 2))
    edges = edges_to_peers(plane_in[:, :, 0].T, plane_in[:, :, -1].T, me, peers)
    sums = jnp.concatenate([own_mean[None], own_square[None], jnp.zeros((6, channels), jnp.float32)])
    payload = jnp.concatenate([jnp.broadcast_to(sums[None], (peers, 8, channels)), edges], axis=1)
    received = lax.all_to_all(payload, "chan", 0, 0, tiled=True)
    means = received[:, 0].reshape(peers, GROUPS, -1)
    squares = received[:, 1].reshape(peers, GROUPS, -1)
    center = jnp.mean(means, axis=(0, 2))
    spread = (jnp.sum(squares, axis=(0, 2)) + pixels * jnp.sum(jnp.square(means - center[None, :, None]), axis=(0, 2))) / count
    inv_spread = lax.rsqrt(spread + 1e-05)
    per_channel = lambda g: jnp.repeat(g, channels // GROUPS)
    center, inv_spread = per_channel(center), per_channel(inv_spread)

    def shape_plane(plane):
        ones = (1,) * (plane.ndim - 1)
        col = lambda v: v.reshape((channels,) + ones)
        normed = (plane - col(center)) * col(inv_spread)
        return normed, normed * col(norm_gain) + col(norm_shift)

    normed, shaped = shape_plane(plane_in)
    active = jax.nn.silu(shaped).astype(jnp.bfloat16)

    def halo_active(step):
        column = edge_of(received[:, 8:], me, peers, step).T
        inside = (me + step >= 0) & (me + step < peers)
        return jnp.where(inside, jax.nn.silu(shape_plane(column)[1]), 0.0).astype(jnp.bfloat16)

    act_padded = padded_plane(active, halo_active(-1), halo_active(1))
    preact = jnp.zeros((channels, pixels), jnp.float32)
    for stencil in range(9):
        preact = preact + jnp.dot(
            spatial_weight[stencil], tap(act_padded, stencil, rows, cols, False), preferred_element_type=jnp.float32
        )
    preact = preact + spatial_bias[:, None]
    hidden = jax.nn.silu(preact).astype(jnp.bfloat16)
    hidden_cross = lax.ppermute(hidden, "frame", neighbour(frames))
    hidden_mate = lax.ppermute(hidden, "frame", partner(1, frames))

    low, mid, high = temporal_weight
    even = core == 0
    ahead = jnp.where(even, low, high)
    behind = jnp.where(even, high, low)
    back_grad = jnp.zeros((channels, pixels), jnp.float32)
    for weight, grad in ((mid, grad_out), (ahead, grad_mate), (behind, grad_cross)):
        back_grad = back_grad + lax.dot_general(weight, grad, CONTRACT_FIRST, preferred_element_type=jnp.float32)
    grad_pre = (back_grad * silu_slope(preact)).astype(jnp.bfloat16)
    own, mate, cross = [
        lax.dot_general(grad, hidden, CONTRACT_LAST, preferred_element_type=jnp.float32)
        for grad in (grad_out, grad_mate, grad_cross)
    ]
    weight_terms = [
        lax.dot_general(grad_pre, tap(act_padded, stencil, rows, cols, False), CONTRACT_LAST, preferred_element_type=jnp.float32)
        for stencil in range(9)
    ]
    weight_terms += [jnp.where(even, mate, cross), own, jnp.where(even, cross, mate)]
    terms = jnp.stack(weight_terms).reshape(peers, 2, -1, channels)
    take = lambda half: lax.dynamic_index_in_dim(terms, half, 1, keepdims=False)
    halves = take(core) + lax.ppermute(take(1 - core), "frame", partner(1, frames))

    grad_plane = grad_pre.reshape(channels, rows, cols)
    edges = edges_to_peers(grad_plane[:, :, 0].T, grad_plane[:, :, -1].T, me, peers).astype(jnp.float32)
    part_rows = halves.shape[1]
    received = lax.all_to_all(jnp.concatenate([halves, edges], axis=1), "chan", 0, 0, tiled=True)
    piece = jnp.sum(received[:, :part_rows], axis=0)
    for near, far in ((2, 4), (8, 16)):
        one, two, three = [lax.ppermute(piece, "frame", partner(bits, frames)) for bits in (near, far, near | far)]
        piece = (piece + one) + (two + three)
    other = lax.ppermute(piece, "frame", partner(1, frames))

    halo_grad = lambda step: edge_of(received[:, part_rows:], me, peers, step).T.astype(jnp.bfloat16)
    grad_padded = padded_plane(grad_plane, halo_grad(-1), halo_grad(1))
    input_part = jnp.zeros((channels, pixels), jnp.float32)
    for stencil in range(9):
        input_part = input_part + lax.dot_general(
            spatial_weight[stencil],
            tap(grad_padded, stencil, rows, cols, True),
            CONTRACT_FIRST,
            preferred_element_type=jnp.float32,
        )
    grad_field = input_part.reshape(channels, rows, cols) * silu_slope(shaped)
    scaled = grad_field * norm_gain[:, None, None]
    sums = jnp.stack([jnp.sum(scaled, axis=(1, 2)), jnp.sum(scaled * normed, axis=(1, 2))])
    sums = jnp.pad(sums, ((0, 6), (0, 0)))

    last = jnp.concatenate([jnp.where(even, piece, other), jnp.where(even, other, piece), sums])
    received = lax.all_to_all(jnp.broadcast_to(last[None], (peers,) + last.shape), "chan", 0, 0, tiled=True)
    weights = received[:, : 2 * part_rows].reshape(12, channels, channels)
    group_sums = jnp.sum(received[:, 2 * part_rows :][:, :2].reshape(peers, 2, GROUPS, -1), axis=(0, 3)) / count
    mean_grad, second = [per_channel(g)[:, None, None] for g in group_sums]
    group_term = inv_spread[:, None, None] * (scaled - mean_grad - normed * second)
    input_grad = (cotangent[0].astype(jnp.float32) + group_term).astype(jnp.bfloat16)

    mixed = jnp.zeros((channels, pixels), jnp.float32)
    ahead = jnp.where(even, high, low)
    behind = jnp.where(even, low, high)
    for weight, frame in ((mid, hidden), (ahead, hidden_mate), (behind, hidden_cross)):
        mixed = mixed + jnp.dot(weight, frame, preferred_element_type=jnp.float32)
    output = (plane_in + mixed.reshape(channels, rows, cols)).astype(jnp.bfloat16)
    return (output[None], input_grad[None], weights[:9], weights[9:])


def solution(mesh):
    banded = P("frame", None, None, "chan")
    return jax.shard_map(
        body,
        mesh=mesh,
        in_specs=(banded, banded, P(), P(), P(), P(), P()),
        out_specs=(banded, banded, P(), P()),
        check_vma=False,
    )
```

```python
import functools

import jax
import jax.numpy as jnp
from jax import lax
from jax.experimental import pallas as pl
from jax.experimental.pallas import tpu as pltpu
from jax.sharding import PartitionSpec as P

GROUPS = 32
LANES = 128
TILE = 512
MIB = 1024 * 1024
CONTRACT_LAST = (((1,), (1,)), ((), ()))
F32, BF16 = jnp.float32, jnp.bfloat16


def partner(bits, frames):
    return [(f, f ^ bits) for f in range(frames)]


def both(frame_bits, chan_bits, frames, peers):
    return [(f * peers + c, (f ^ frame_bits) * peers + (c ^ chan_bits)) for f in range(frames) for c in range(peers)]


def neighbour(frames):
    pairs = []
    for f in range(frames):
        target = f + 1 if f % 2 else f - 1
        if 0 <= target < frames:
            pairs.append((f, target))
    return pairs


def call(kernel, outs, ins, scratch=(), cost=(0, 0), limit=24):
    smem = pl.BlockSpec(memory_space=pltpu.SMEM)
    vmem = pl.BlockSpec(memory_space=pltpu.VMEM)
    is_place = lambda v: v.dtype == jnp.int32
    flops, moved = cost
    return pl.pallas_call(
        kernel,
        out_shape=[jax.ShapeDtypeStruct(s, d) for s, d in outs],
        in_specs=[smem if is_place(v) else vmem for v in ins],
        out_specs=[vmem] * len(outs),
        scratch_shapes=list(scratch),
        cost_estimate=pl.CostEstimate(flops=flops, bytes_accessed=moved, transcendentals=0),
        compiler_params=pltpu.CompilerParams(vmem_limit_bytes=limit * MIB),
    )(*ins)


def lane_index(shape=(LANES, LANES)):
    return lax.broadcasted_iota(jnp.int32, shape, len(shape) - 1)


def row_at(r):
    return pl.ds(pl.multiple_of(r * LANES, LANES), LANES)


def tile_at(n, extra=0):
    return pl.ds(pl.multiple_of(n * TILE, LANES) + extra, TILE)


def group_sum(v):
    lane = lax.broadcasted_iota(jnp.int32, v.shape, 1)
    for step in (1, 2):
        up, down = pltpu.roll(v, LANES - step, 1), pltpu.roll(v, step, 1)
        v = v + jnp.where((lane // step) % 2 == 0, up, down)
    return v


def sigmoid(v):
    return 1.0 / (1.0 + jnp.exp(-v))


def selector(n, rows):
    pixel = lax.broadcasted_iota(jnp.int32, (LANES, TILE), 1) + n * TILE
    at = lax.broadcasted_iota(jnp.int32, (LANES, TILE), 0)
    low = (at < rows) & (pixel == at * LANES)
    high = (at >= 64) & (pixel == (at - 64) * LANES + (LANES - 1))
    return jnp.where(low | high | (at == 32), 1.0, 0.0).astype(BF16)


def turn(raw):
    return jnp.swapaxes(raw, 0, 1)


def store_shifts(ref, row, halo, r, lane, order):
    left = jnp.where(lane == 0, pltpu.roll(halo, LANES - 32 - r, 1), pltpu.roll(row, 1, 1))
    right = jnp.where(lane == LANES - 1, pltpu.roll(halo, 63 - r, 1), pltpu.roll(row, LANES - 1, 1))
    shifts = (left, row, right)
    for slot, which in enumerate(order):
        ref[slot * LANES : (slot + 1) * LANES, row_at(r + 1)] = shifts[which].astype(BF16)


def turn_kernel(raw_ref, low_ref, high_ref):
    channels, rows, _ = raw_ref.shape
    for c in range(0, channels, 16):
        block = turn(raw_ref[c : c + 16])
        for r in range(rows):
            ref, at = (low_ref, r) if r < rows // 2 else (high_ref, r - rows // 2)
            ref[c : c + 16, at * LANES : (at + 1) * LANES] = block[r]


def sums_kernel(me_ref, raw_ref, out_ref, payload_ref):
    channels, rows, _ = raw_ref.shape
    me = me_ref[0]
    for c in range(0, channels, 16):
        block = turn(raw_ref[c : c + 16])
        for r in range(rows):
            out_ref[c : c + 16, r * LANES : (r + 1) * LANES] = block[r]
    packed = jnp.zeros((LANES, channels), F32)
    for n in range(rows * LANES // TILE):
        packed += lax.dot_general(selector(n, rows), out_ref[:, n * TILE : (n + 1) * TILE], CONTRACT_LAST, preferred_element_type=F32)
    mean = packed[32:33] / (rows * LANES)
    mean_all = jnp.broadcast_to(mean, (LANES, channels)).T

    def square(r, acc):
        off = out_ref[:, row_at(r)].astype(F32) - mean_all
        return acc + off * off

    squares = lax.fori_loop(0, rows, square, jnp.zeros((channels, LANES), F32), unroll=4)
    squares = jnp.sum(squares.T, axis=0, keepdims=True)
    head = jnp.concatenate([mean, squares, jnp.zeros((6, channels), F32)], axis=0)
    for peer in range(payload_ref.shape[0]):
        payload_ref[peer, 0:8, :] = head
        payload_ref[peer, 8 : 8 + rows, :] = jnp.where(peer < me, packed[0:rows], packed[64 : 64 + rows])


def forward_kernel(me_ref, plane_ref, received_ref, table_ref, weight_ref, act_ref, hidden_ref, slope_ref, columns_ref):
    channels, pixels = plane_ref.shape
    rows = pixels // LANES
    peers = received_ref.shape[0]
    me = me_ref[0]
    lane = lane_index()
    count = (channels // GROUPS) * pixels * peers
    means, squares = received_ref[:, 0, :], received_ref[:, 1, :]
    center = group_sum(jnp.sum(means, axis=0, keepdims=True)) * (GROUPS / (channels * peers))
    off = means - center
    spread = group_sum(jnp.sum(squares + pixels * (off * off), axis=0, keepdims=True)) / count
    inverse = lax.rsqrt(spread + 1e-05)
    low = received_ref[jnp.maximum(me - 1, 0), 8 : 8 + rows, :]
    high = received_ref[jnp.minimum(me + 1, peers - 1), 8 : 8 + rows, :]
    head = jnp.concatenate([center, inverse, table_ref[0:6, :]], axis=0)
    gap = jnp.zeros((24, LANES), F32)
    columns = jnp.concatenate([head, gap, low, high, jnp.zeros((32, LANES), F32)], axis=0).T
    columns_ref[...] = columns
    wide = lambda at: jnp.broadcast_to(columns[:, at : at + 1], (channels, LANES))
    center_w, inverse_w, gain_w, shift_w, bias_w = [wide(at) for at in range(5)]

    def activate(v):
        v = (v - center_w) * inverse_w * gain_w + shift_w
        return v * sigmoid(v)

    inside = ((lane < 64) & (me > 0)) | ((lane >= 64) & (me < peers - 1))
    halo = jnp.where(inside, activate(columns), 0.0)
    nothing = jnp.zeros((3 * channels, LANES), BF16)
    act_ref[:, 0:LANES] = nothing
    act_ref[:, (rows + 1) * LANES : (rows + 2) * LANES] = nothing

    def shape_row(r, carry):
        row = activate(plane_ref[:, row_at(r)].astype(F32))
        store_shifts(act_ref, row, halo, r, lane, (0, 1, 2))
        return carry

    lax.fori_loop(0, rows, shape_row, 0, unroll=2)
    weights = [jnp.concatenate([weight_ref[3 * dy + dx] for dx in range(3)], axis=1) for dy in range(3)]
    bias = jnp.broadcast_to(bias_w[:, 0:1], (channels, TILE))

    def conv(n, carry):
        value = bias
        for dy in range(3):
            value = value + jnp.dot(weights[dy], act_ref[:, tile_at(n, dy * LANES)], preferred_element_type=F32)
        logistic = sigmoid(value)
        hidden_ref[:, tile_at(n)] = (value * logistic).astype(BF16)
        slope_ref[:, tile_at(n)] = logistic * (1.0 + value * (1.0 - logistic))
        return carry

    lax.fori_loop(0, pixels // TILE, conv, 0)


def backward_kernel(last, me_ref, act_ref, hidden_ref, slope_ref, grad_ref, mate_ref, cross_ref, weight_ref, *rest):
    if last:
        early_in, late_in, packed_in, pre_ref, terms_ref, low_ref, high_ref, early, late = rest
    else:
        pre_ref, early, late, packed_ref = rest
    channels, pixels = grad_ref.shape
    rows = 2 * pixels // LANES
    core, spot = me_ref[1], me_ref[2]
    first = pixels // TILE if last else 0
    turned = [weight_ref[k].astype(F32).T for k in range(3)]
    even = core == 0
    ahead = jnp.where(even, turned[0], turned[2])
    behind = jnp.where(even, turned[2], turned[0])
    weights = jnp.concatenate([turned[1], ahead, behind], axis=1).astype(BF16)
    early[...] = early_in[...] if last else jnp.zeros(early.shape, F32)
    late[...] = late_in[...] if last else jnp.zeros(late.shape, F32)

    def step(n, packed):
        whole = n + first
        grads = jnp.concatenate([ref[:, tile_at(n)] for ref in (grad_ref, mate_ref, cross_ref)], axis=0)
        back = jnp.dot(weights, grads, preferred_element_type=F32)
        pre = (back * slope_ref[:, tile_at(whole)]).astype(BF16)
        pre_ref[:, tile_at(n)] = pre
        early[...] += lax.dot_general(grads, hidden_ref[:, tile_at(whole)], CONTRACT_LAST, preferred_element_type=F32)
        for dy in range(3):
            late[dy] += lax.dot_general(pre, act_ref[:, tile_at(whole, dy * LANES)], CONTRACT_LAST, preferred_element_type=F32)
        return packed + lax.dot_general(selector(whole, rows), pre, CONTRACT_LAST, preferred_element_type=F32)

    packed = lax.fori_loop(0, pixels // TILE, step, packed_in[...] if last else jnp.zeros((LANES, channels), F32))
    if not last:
        packed_ref[...] = packed
        return
    low_ref[...] = packed[0:rows]
    high_ref[...] = packed[64 : 64 + rows]
    own, mate, cross = [early[i * channels : (i + 1) * channels, :] for i in range(3)]
    blocks = [late[t // 3, :, (t % 3) * LANES : (t % 3 + 1) * LANES] for t in range(9)]
    blocks += [jnp.where(even, mate, cross), own, jnp.where(even, cross, mate)]
    part = terms_ref.shape[2]
    for t, block in enumerate(blocks):
        for v in range(channels // 64):
            at = (t * channels + v * 64) // part
            offset = (t * channels + v * 64) % part
            half = jnp.where(core == at % 2, 0, 1)
            terms_ref[half, at // 2 ^ spot, offset : offset + 64, :] = block[v * 64 : (v + 1) * 64]


def input_kernel(early_ref, late_ref, low_ref, high_ref, weight_ref, plane_ref, columns_ref, scaled_ref, sums_ref, padded):
    channels, pixels = plane_ref.shape
    rows = pixels // LANES
    lane = lane_index()
    blank = jnp.zeros((32, LANES), F32)
    halo = jnp.concatenate([blank, low_ref[...], high_ref[...], blank], axis=0).T
    nothing = jnp.zeros((3 * channels, LANES), BF16)
    padded[:, 0:LANES] = nothing
    padded[:, (rows + 1) * LANES : (rows + 2) * LANES] = nothing

    for first, ref in ((0, early_ref), (rows // 2, late_ref)):

        def shift_row(r, carry, ref=ref, first=first):
            store_shifts(padded, ref[:, row_at(r)].astype(F32), halo, r + first, lane, (2, 1, 0))
            return carry

        lax.fori_loop(0, rows // 2, shift_row, 0, unroll=2)
    weights = [
        jnp.concatenate([weight_ref[3 * dy + dx].astype(F32).T for dx in range(3)], axis=1).astype(BF16) for dy in range(3)
    ]
    columns = columns_ref[...]
    wide = lambda at: jnp.broadcast_to(columns[:, at : at + 1], (channels, LANES))
    center, inverse, gain, shift = [wide(at) for at in range(4)]

    def step(n, carry):
        plain, crossed = carry
        value = jnp.zeros((channels, TILE), F32)
        for dy in range(3):
            value = value + jnp.dot(weights[dy], padded[:, tile_at(n, (2 - dy) * LANES)], preferred_element_type=F32)
        for i in range(TILE // LANES):
            at = row_at(n * (TILE // LANES) + i)
            normed = (plane_ref[:, at].astype(F32) - center) * inverse
            shaped = normed * gain + shift
            logistic = sigmoid(shaped)
            field = value[:, i * LANES : (i + 1) * LANES] * (logistic * (1.0 + shaped * (1.0 - logistic)))
            scaled = field * gain
            scaled_ref[:, at] = scaled
            plain, crossed = plain + scaled, crossed + scaled * normed
        return plain, crossed

    zero = jnp.zeros((channels, LANES), F32)
    plain, crossed = lax.fori_loop(0, pixels // TILE, step, (zero, zero))
    plain, crossed = [jnp.sum(v, axis=1, keepdims=True) for v in (plain, crossed)]
    sums_ref[...] = jnp.where(lane == 0, plain, jnp.where(lane == 1, crossed, 0.0)).T[0:8]


def output_kernel(me_ref, hidden_ref, mate_ref, cross_ref, weight_ref, raw_ref, out_ref, flat):
    channels, rows, _ = raw_ref.shape
    even = me_ref[1] == 0
    pick = lambda a, b: jnp.where(even, weight_ref[a].astype(F32), weight_ref[b].astype(F32)).astype(BF16)
    weights = jnp.concatenate([weight_ref[1], pick(2, 0), pick(0, 2)], axis=1)
    each = TILE // LANES

    def step(n, carry):
        frames = jnp.concatenate([ref[:, tile_at(n)] for ref in (hidden_ref, mate_ref, cross_ref)], axis=0)
        mixed = jnp.dot(weights, frames, preferred_element_type=F32)
        for i in range(each):
            flat[n * each + i] = mixed[:, i * LANES : (i + 1) * LANES]
        return carry

    lax.fori_loop(0, rows // each, step, 0)
    for c in range(0, channels, 16):
        out_ref[c : c + 16] = (raw_ref[c : c + 16].astype(F32) + turn(flat[:, c : c + 16, :])).astype(BF16)


def final_kernel(own_ref, one_ref, two_ref, three_ref, scaled_ref, plane_ref, columns_ref, raw_ref, out_ref, flat):
    channels, rows, _ = raw_ref.shape
    count = (channels // GROUPS) * rows * LANES * 8
    at = own_ref.shape[0] - 8
    totals = (own_ref[at:, :] + one_ref[at:, :]) + (two_ref[at:, :] + three_ref[at:, :])
    totals = group_sum(totals) / count
    turned = jnp.concatenate([totals, jnp.zeros((LANES - 8, LANES), F32)], axis=0).T
    wide = lambda v, at: jnp.broadcast_to(v[:, at : at + 1], (channels, LANES))
    mean_grad, second = wide(turned, 0), wide(turned, 1)
    columns = columns_ref[...]
    center, inverse = wide(columns, 0), wide(columns, 1)

    def step(r, carry):
        normed = (plane_ref[:, row_at(r)].astype(F32) - center) * inverse
        flat[r] = inverse * (scaled_ref[:, row_at(r)] - mean_grad - normed * second)
        return carry

    lax.fori_loop(0, rows, step, 0, unroll=2)
    for c in range(0, channels, 16):
        out_ref[c : c + 16] = (raw_ref[c : c + 16].astype(F32) + turn(flat[:, c : c + 16, :])).astype(BF16)


def place_kernel(me_ref, own_ref, mate_ref, spatial_ref, temporal_ref, whole):
    core, spot = me_ref[1], me_ref[2]
    part = whole.shape[1]
    for slot in range(4):
        at = 2 * (slot ^ spot)
        whole[at + core] = own_ref[slot, 0:part]
        whole[at + 1 - core] = mate_ref[slot, 0:part]
    split = spatial_ref.shape[0] // part
    spatial_ref[...] = whole[0:split].reshape(spatial_ref.shape)
    temporal_ref[...] = whole[split:].reshape(temporal_ref.shape)


def body(inputs, cotangent, spatial_weight, temporal_weight, norm_gain, norm_shift, spatial_bias):
    frames = lax.axis_size("frame")
    peers = lax.axis_size("chan")
    core = lax.axis_index("frame") % 2
    me = lax.axis_index("chan")
    channels, rows, cols = inputs.shape[1:]
    pixels = rows * cols
    plane, half = (channels, pixels), (channels, pixels // 2)
    tied = lax.optimization_barrier
    place = jnp.stack([me, core, me // 2]).astype(jnp.int32)
    table = jnp.pad(jnp.stack([norm_gain, norm_shift, spatial_bias]), ((0, 5), (0, 0)))
    raw_in, raw_grad = inputs[0], cotangent[0]
    cross = lambda v: lax.ppermute(v, "frame", neighbour(frames))
    mate = lambda v: lax.ppermute(v, "frame", partner(1, frames))

    def meet(v, frame_bits, chan_bits):
        return lax.ppermute(v, ("frame", "chan"), both(frame_bits, chan_bits, frames, peers))

    def total(v, steps):
        got = [v] + [meet(v, *step) for step in steps]
        return got[0] + got[1] if len(got) == 2 else (got[0] + got[1]) + (got[2] + got[3])

    grads = call(turn_kernel, [(half, BF16)] * 2, [raw_grad], cost=(0, 2 * MIB), limit=8)
    raw_in, early_grad, table, place = tied((raw_in, grads[0], table, place))
    crossed = [cross(early_grad)]
    turned, payload = call(
        sums_kernel, [(plane, BF16), ((peers, 8 + rows, channels), F32)], [place, raw_in], cost=(0, 2 * MIB), limit=8
    )
    received = lax.all_to_all(payload, "chan", 0, 0, tiled=True)
    early_grad, late_grad, received = tied((early_grad, grads[1], received))
    grads = [early_grad, late_grad]
    crossed.append(cross(late_grad))
    mates = [mate(v) for v in grads]

    padded = (3 * channels, pixels + 2 * cols)
    act, hidden, slope, columns = call(
        forward_kernel,
        [(padded, BF16), (plane, BF16), (plane, F32), ((channels, LANES), F32)],
        [place, turned, received, table, spatial_weight],
        cost=(1000, MIB),
        limit=16,
    )
    early_shape, late_shape = (3 * channels, channels), (3, channels, 3 * channels)
    pre_early, *sums = call(
        functools.partial(backward_kernel, False),
        [(half, BF16), (early_shape, F32), (late_shape, F32), ((LANES, channels), F32)],
        [place, act, hidden, slope, grads[0], mates[0], crossed[0], temporal_weight],
        cost=(1000, MIB),
        limit=16,
    )
    sent, late_cross = tied((hidden, crossed[1]))
    hidden_cross, hidden_mate = cross(sent), mate(sent)
    part = 12 * channels // 8
    edge = ((rows, channels), F32)
    pre_late, terms, low, high = call(
        functools.partial(backward_kernel, True),
        [(half, BF16), ((2, 4, part, channels), F32), edge, edge],
        [place, act, hidden, slope, grads[1], mates[1], late_cross, temporal_weight, *sums],
        [pltpu.VMEM(early_shape, F32), pltpu.VMEM(late_shape, F32)],
        cost=(1000, MIB),
        limit=16,
    )
    terms = terms[0] + mate(terms[1])
    got = [terms[0]] + [meet(terms[b], 0, 2 * b) for b in (1, 2, 3)]
    piece = (got[0] + got[1]) + (got[2] + got[3])
    ups, downs = [(c, c + 1) for c in range(peers - 1)], [(c + 1, c) for c in range(peers - 1)]
    halo_low, halo_high = lax.ppermute(high, "chan", ups), lax.ppermute(low, "chan", downs)
    piece = total(piece, [(4, 0), (8, 0), (12, 0)])
    piece = total(piece, [(16, 0)])
    piece, hidden_cross, hidden_mate = tied((piece, hidden_cross, hidden_mate))
    scaled, sums = call(
        input_kernel,
        [(plane, F32), ((8, channels), F32)],
        [pre_early, pre_late, halo_low, halo_high, spatial_weight, turned, columns],
        [pltpu.VMEM(padded, BF16)],
        cost=(18 * channels * channels * pixels, 6 * MIB),
        limit=16,
    )
    sums = total(sums, [(0, 1)])
    piece = total(piece, [(2, 0), (0, 1), (2, 1)])
    flat = pltpu.VMEM((rows, channels, cols), F32)
    (output,) = call(
        output_kernel,
        [(raw_in.shape, BF16)],
        [place, hidden, hidden_mate, hidden_cross, temporal_weight, raw_in],
        [flat],
        cost=(6 * channels * channels * pixels, 5 * MIB),
        limit=16,
    )
    piece = jnp.concatenate([piece, sums])
    got = [piece] + [meet(piece, 0, 2 * b) for b in (1, 2, 3)]
    own = jnp.stack(got)
    other = mate(own)
    (input_grad,) = call(
        final_kernel,
        [(raw_in.shape, BF16)],
        [*got, scaled, turned, columns, raw_grad],
        [flat],
        cost=(0, 5 * MIB),
        limit=16,
    )
    spatial_grad, temporal_grad = call(
        place_kernel,
        [((9 * channels, channels), F32), ((3 * channels, channels), F32)],
        [place, own, other],
        [pltpu.VMEM((8, part, channels), F32)],
        cost=(0, MIB),
        limit=8,
    )
    square = (-1, channels, channels)
    return (output[None], input_grad[None], spatial_grad.reshape(square), temporal_grad.reshape(square))


def solution(mesh):
    banded = P("frame", None, None, "chan")
    return jax.shard_map(
        body,
        mesh=mesh,
        in_specs=(banded, banded, P(), P(), P(), P(), P()),
        out_specs=(banded, banded, P(), P()),
        check_vma=False,
    )
```

```python
import functools

import jax
import jax.numpy as jnp
from jax import lax
from jax.experimental import pallas as pl
from jax.experimental.pallas import tpu as pltpu
from jax.sharding import PartitionSpec as P

GROUPS = 32
LANES = 128
TILE = 1024
MIB = 1024 * 1024
CONTRACT_LAST = (((1,), (1,)), ((), ()))
F32, BF16 = jnp.float32, jnp.bfloat16


def partner(bits, frames):
    return [(f, f ^ bits) for f in range(frames)]


def both(frame_bits, chan_bits, frames, peers):
    return [(f * peers + c, (f ^ frame_bits) * peers + (c ^ chan_bits)) for f in range(frames) for c in range(peers)]


def crossing(frames, inside):
    return [(f, t) for f, t in neighbour(frames) if (f // 4 == t // 4) == inside]


def neighbour(frames):
    pairs = []
    for f in range(frames):
        target = f + 1 if f % 2 else f - 1
        if 0 <= target < frames:
            pairs.append((f, target))
    return pairs


def call(kernel, outs, ins, scratch=(), cost=(0, 0), limit=24):
    smem = pl.BlockSpec(memory_space=pltpu.SMEM)
    vmem = pl.BlockSpec(memory_space=pltpu.VMEM)
    is_place = lambda v: v.dtype == jnp.int32
    flops, moved = cost
    return pl.pallas_call(
        kernel,
        out_shape=[jax.ShapeDtypeStruct(s, d) for s, d in outs],
        in_specs=[smem if is_place(v) else vmem for v in ins],
        out_specs=[vmem] * len(outs),
        scratch_shapes=list(scratch),
        cost_estimate=pl.CostEstimate(flops=flops, bytes_accessed=moved, transcendentals=0),
        compiler_params=pltpu.CompilerParams(vmem_limit_bytes=limit * MIB),
    )(*ins)


def lane_index(shape=(LANES, LANES)):
    return lax.broadcasted_iota(jnp.int32, shape, len(shape) - 1)


def row_at(r):
    return pl.ds(pl.multiple_of(r * LANES, LANES), LANES)


def span(row, rows):
    return slice(row * LANES, (row + rows) * LANES)


def side(parts):
    return jnp.concatenate(parts, axis=1)


def tile_at(n, extra=0):
    return pl.ds(pl.multiple_of(n * TILE, LANES) + extra, TILE)


def group_sum(v):
    lane = lax.broadcasted_iota(jnp.int32, v.shape, 1)
    for step in (1, 2):
        up, down = pltpu.roll(v, LANES - step, 1), pltpu.roll(v, step, 1)
        v = v + jnp.where((lane // step) % 2 == 0, up, down)
    return v


def sigmoid(v):
    return 1.0 / (1.0 + jnp.exp(-v))


def selector(n, rows):
    pixel = lax.broadcasted_iota(jnp.int32, (LANES, TILE), 1) + n * TILE
    at = lax.broadcasted_iota(jnp.int32, (LANES, TILE), 0)
    low = (at < rows) & (pixel == at * LANES)
    high = (at >= 64) & (pixel == (at - 64) * LANES + (LANES - 1))
    return jnp.where(low | high | (at == 32), 1.0, 0.0).astype(BF16)


def turn(raw):
    return jnp.swapaxes(raw, 0, 1)


def store_shifts(ref, row, halo, r, lane, order, offset=1):
    row = row.astype(BF16)
    left = jnp.where(lane == 0, pltpu.roll(halo, LANES - 32 - r, 1), pltpu.roll(row, 1, 1))
    right = jnp.where(lane == LANES - 1, pltpu.roll(halo, 63 - r, 1), pltpu.roll(row, LANES - 1, 1))
    shifts = (left, row, right)
    for slot, which in enumerate(order):
        ref[slot * LANES : (slot + 1) * LANES, row_at(r + offset)] = shifts[which].astype(BF16)


def turn_kernel(raw_ref, low_ref, high_ref):
    channels, rows, _ = raw_ref.shape
    for c in range(0, channels, 16):
        block = turn(raw_ref[c : c + 16])
        for r in range(rows):
            ref, at = (low_ref, r) if r < rows // 2 else (high_ref, r - rows // 2)
            ref[c : c + 16, at * LANES : (at + 1) * LANES] = block[r]


def sums_kernel(me_ref, raw_ref, out_ref, payload_ref):
    channels, rows, _ = raw_ref.shape
    me = me_ref[0]
    for c in range(0, channels, 16):
        block = turn(raw_ref[c : c + 16])
        for r in range(rows):
            out_ref[c : c + 16, r * LANES : (r + 1) * LANES] = block[r]
    packed = jnp.zeros((LANES, channels), F32)
    for n in range(rows * LANES // TILE):
        packed += lax.dot_general(selector(n, rows), out_ref[:, n * TILE : (n + 1) * TILE], CONTRACT_LAST, preferred_element_type=F32)
    mean = packed[32:33] / (rows * LANES)
    mean_all = jnp.broadcast_to(mean, (LANES, channels)).T

    def square(r, acc):
        off = out_ref[:, row_at(r)].astype(F32) - mean_all
        return acc + off * off

    squares = lax.fori_loop(0, rows, square, jnp.zeros((channels, LANES), F32), unroll=4)
    squares = jnp.sum(squares.T, axis=0, keepdims=True)
    head = jnp.concatenate([mean, squares, jnp.zeros((6, channels), F32)], axis=0)
    for peer in range(payload_ref.shape[0]):
        payload_ref[peer, 0:8, :] = head
        payload_ref[peer, 8 : 8 + rows, :] = jnp.where(peer < me, packed[0:rows], packed[64 : 64 + rows])


def forward_kernel(me_ref, plane_ref, received_ref, table_ref, weight_ref, act_ref, hidden_ref, slope_ref, columns_ref):
    channels, pixels = plane_ref.shape
    rows = pixels // LANES
    peers = received_ref.shape[0]
    me = me_ref[0]
    lane = lane_index()
    count = (channels // GROUPS) * pixels * peers
    means, squares = received_ref[:, 0, :], received_ref[:, 1, :]
    center = group_sum(jnp.sum(means, axis=0, keepdims=True)) * (GROUPS / (channels * peers))
    off = means - center
    spread = group_sum(jnp.sum(squares + pixels * (off * off), axis=0, keepdims=True)) / count
    inverse = lax.rsqrt(spread + 1e-05)
    low = received_ref[jnp.maximum(me - 1, 0), 8 : 8 + rows, :]
    high = received_ref[jnp.minimum(me + 1, peers - 1), 8 : 8 + rows, :]
    head = jnp.concatenate([center, inverse, table_ref[...], jnp.zeros((3, LANES), F32)], axis=0)
    gap = jnp.zeros((24, LANES), F32)
    columns = jnp.concatenate([head, gap, low, high, jnp.zeros((32, LANES), F32)], axis=0).T
    columns_ref[...] = columns
    wide = lambda at: jnp.broadcast_to(columns[:, at : at + 1], (channels, LANES))
    center_w, inverse_w, gain_w, shift_w, bias_w = [wide(at) for at in range(5)]

    def activate(v):
        v = (v - center_w) * inverse_w * gain_w + shift_w
        return v * sigmoid(v)

    inside = ((lane < 64) & (me > 0)) | ((lane >= 64) & (me < peers - 1))
    halo = jnp.where(inside, activate(columns), 0.0).astype(BF16)
    nothing = jnp.zeros((3 * channels, LANES), BF16)
    act_ref[:, 0:LANES] = nothing
    act_ref[:, (rows + 1) * LANES : (rows + 2) * LANES] = nothing

    def shape_row(r, carry):
        row = activate(plane_ref[:, row_at(r)].astype(F32))
        store_shifts(act_ref, row, halo, r, lane, (0, 1, 2))
        return carry

    lax.fori_loop(0, rows, shape_row, 0, unroll=8)
    weights = side([weight_ref[t] for t in range(9)])
    each = TILE // LANES
    bias = jnp.broadcast_to(bias_w[:, 0:1], (channels, TILE))
    for n in range(rows // each):
        window = jnp.concatenate([act_ref[:, span(n * each + dy, each)] for dy in range(3)], axis=0)
        value = jnp.dot(weights, window, preferred_element_type=F32) + bias
        logistic = sigmoid(value)
        hidden_ref[:, span(n * each, each)] = (value * logistic).astype(BF16)
        slope_ref[:, span(n * each, each)] = logistic * (1.0 + value * (1.0 - logistic))


def backward_kernel(last, me_ref, act_ref, hidden_ref, slope_ref, grad_ref, mate_ref, cross_ref, *rest):
    if last:
        weight_ref, early_in, late_in, packed_in, *rest = rest
        pre_ref, keep_ref, send_ref, edges_ref, early, late, shifted = rest
    else:
        weight_ref, pre_ref, early, late, packed_ref, shifted = rest
    channels, pixels = grad_ref.shape
    rows = 2 * pixels // LANES
    core, spot = me_ref[1], me_ref[2]
    turned = [weight_ref[k].astype(F32).T for k in range(3)]
    even = core == 0
    ahead = jnp.where(even, turned[0], turned[2])
    behind = jnp.where(even, turned[2], turned[0])
    weights = jnp.concatenate([turned[1], ahead, behind], axis=1).astype(BF16)
    own_rows = rows // 2
    start = own_rows if last else 0
    blank = jnp.zeros((channels, 2 * LANES), BF16)
    shifted[:, span(0, 2)] = blank
    shifted[:, span(own_rows + 2, 2)] = blank
    each = TILE // LANES
    fresh = jnp.zeros((3 * channels, channels), F32)
    packed = jnp.zeros((LANES, channels), F32)
    for n in range(own_rows // each):
        at, whole = span(n * each, each), span(n * each + start, each)
        grads = jnp.concatenate([ref[:, at] for ref in (grad_ref, mate_ref, cross_ref)], axis=0)
        back = jnp.dot(weights, grads, preferred_element_type=F32)
        pre = (back * slope_ref[:, whole]).astype(BF16)
        pre_ref[:, at] = pre
        shifted[:, span(n * each + 2, each)] = pre
        fresh += lax.dot_general(grads, hidden_ref[:, whole], CONTRACT_LAST, preferred_element_type=F32)
        packed += lax.dot_general(selector(n + start // each, rows), pre, CONTRACT_LAST, preferred_element_type=F32)
    lhs = jnp.concatenate([shifted[:, span(2 - dy, own_rows + 2)] for dy in range(3)], axis=0)
    rhs = act_ref[:, span(start, own_rows + 2)]
    latest = lax.dot_general(lhs, rhs, CONTRACT_LAST, preferred_element_type=F32)
    early[...] = fresh + early_in[...] if last else fresh
    late[...] = latest + late_in[...] if last else latest
    packed = packed + packed_in[...] if last else packed
    if not last:
        packed_ref[...] = packed
        return
    low, high = packed[0:rows], packed[64 : 64 + rows]
    left = me_ref[0] % 2 == 0
    edges_ref[0:rows, :] = jnp.where(left, high, low)
    edges_ref[rows:, :] = jnp.where(left, low, high)
    own, mate, cross = [early[i * channels : (i + 1) * channels, :] for i in range(3)]
    blocks = [late[t // 3 * channels : (t // 3 + 1) * channels, span(t % 3, 1)] for t in range(9)]
    blocks += [jnp.where(even, mate, cross), own, jnp.where(even, cross, mate)]
    part = keep_ref.shape[1]

    def rows_at(at):
        return blocks[at // channels][at % channels : at % channels + 64]

    for y in range(4):
        slot = y ^ spot
        for v in range(0, part, 64):
            one, two = rows_at(2 * y * part + v), rows_at((2 * y + 1) * part + v)
            keep_ref[slot, v : v + 64, :] = jnp.where(even, one, two)
            send_ref[slot, v : v + 64, :] = jnp.where(even, two, one)


def input_kernel(me_ref, early_ref, late_ref, near_ref, one_ref, three_ref, *refs):
    weight_ref, plane_ref, columns_ref, scaled_ref, sums_ref, padded, total = refs
    channels, pixels = plane_ref.shape
    rows = pixels // LANES
    lane = lane_index()
    blank = jnp.zeros((32, LANES), F32)
    me = me_ref[0]
    left = me % 2 == 0
    near = near_ref[0:rows, :]
    at = one_ref.shape[0] - rows
    far = jnp.where((me // 2 % 2 == 0) != left, one_ref[at:, :], three_ref[at:, :])
    far = jnp.where((me > 0) & (me < 7), far, 0.0)
    low, high = jnp.where(left, far, near), jnp.where(left, near, far)
    halo = jnp.concatenate([blank, low, high, blank], axis=0).T.astype(BF16)
    for first, ref in ((0, early_ref), (rows // 2, late_ref)):

        def shift_row(r, carry, ref=ref, first=first):
            store_shifts(padded, ref[:, row_at(r)], halo, r + first, lane, (2, 1, 0))
            return carry

        lax.fori_loop(0, rows // 2, shift_row, 0, unroll=8)
    flipped = lambda t: weight_ref[t].astype(F32).T.astype(BF16)
    weights = side([flipped(3 * dy + dx) for dy in (2, 1, 0) for dx in range(3)])
    each = TILE // LANES
    padded[:, span(0, 1)] = jnp.zeros((3 * channels, LANES), BF16)
    padded[:, span(rows + 1, 1)] = jnp.zeros((3 * channels, LANES), BF16)
    for n in range(rows // each):
        window = jnp.concatenate([padded[:, span(n * each + dy, each)] for dy in range(3)], axis=0)
        total[:, span(n * each + 1, each)] = jnp.dot(weights, window, preferred_element_type=F32)
    columns = columns_ref[...]
    wide = lambda at: jnp.broadcast_to(columns[:, at : at + 1], (channels, LANES))
    center, inverse, gain, shift = [wide(at) for at in range(4)]

    def step(r, carry):
        plain, crossed = carry
        normed = (plane_ref[:, row_at(r)].astype(F32) - center) * inverse
        shaped = normed * gain + shift
        logistic = sigmoid(shaped)
        scaled = total[:, row_at(r + 1)] * (logistic * (1.0 + shaped * (1.0 - logistic))) * gain
        scaled_ref[:, row_at(r)] = scaled
        return plain + scaled, crossed + scaled * normed

    zero = jnp.zeros((channels, LANES), F32)
    plain, crossed = lax.fori_loop(0, rows, step, (zero, zero), unroll=4)
    plain, crossed = [jnp.sum(v, axis=1, keepdims=True) for v in (plain, crossed)]
    sums_ref[...] = jnp.where(lane == 0, plain, jnp.where(lane == 1, crossed, 0.0)).T[0:8]


def output_kernel(me_ref, hidden_ref, mate_ref, inside_ref, outside_ref, weight_ref, raw_ref, out_ref, flat):
    channels, rows, _ = raw_ref.shape
    inside = me_ref[3] == 1
    even = me_ref[1] == 0
    pick = lambda a, b: jnp.where(even, weight_ref[a].astype(F32), weight_ref[b].astype(F32)).astype(BF16)
    weights = jnp.concatenate([weight_ref[1], pick(2, 0), pick(0, 2)], axis=1)
    each = TILE // LANES

    def step(n, carry):
        across = jnp.where(inside, inside_ref[:, tile_at(n)], outside_ref[:, tile_at(n)])
        frames = jnp.concatenate([hidden_ref[:, tile_at(n)], mate_ref[:, tile_at(n)], across], axis=0)
        mixed = jnp.dot(weights, frames, preferred_element_type=F32)
        for i in range(each):
            flat[n * each + i] = mixed[:, i * LANES : (i + 1) * LANES]
        return carry

    lax.fori_loop(0, rows // each, step, 0, unroll=2)
    for c in range(0, channels, 16):
        out_ref[c : c + 16] = (raw_ref[c : c + 16].astype(F32) + turn(flat[:, c : c + 16, :])).astype(BF16)


def final_kernel(own_ref, one_ref, two_ref, three_ref, scaled_ref, plane_ref, columns_ref, raw_ref, out_ref, flat):
    channels, rows, _ = raw_ref.shape
    count = (channels // GROUPS) * rows * LANES * 8
    at = own_ref.shape[0] - 8
    totals = (own_ref[at:, :] + one_ref[at:, :]) + (two_ref[at:, :] + three_ref[at:, :])
    totals = group_sum(totals) / count
    turned = jnp.concatenate([totals, jnp.zeros((LANES - 8, LANES), F32)], axis=0).T
    wide = lambda v, at: jnp.broadcast_to(v[:, at : at + 1], (channels, LANES))
    mean_grad, second = wide(turned, 0), wide(turned, 1)
    columns = columns_ref[...]
    center, inverse = wide(columns, 0), wide(columns, 1)

    def step(r, carry):
        normed = (plane_ref[:, row_at(r)].astype(F32) - center) * inverse
        flat[r] = inverse * (scaled_ref[:, row_at(r)] - mean_grad - normed * second)
        return carry

    lax.fori_loop(0, rows, step, 0, unroll=2)
    for c in range(0, channels, 16):
        out_ref[c : c + 16] = (raw_ref[c : c + 16].astype(F32) + turn(flat[:, c : c + 16, :])).astype(BF16)


def place_kernel(me_ref, *refs):
    spatial_ref, temporal_ref, whole = refs[8:]
    core, spot = me_ref[1], me_ref[2]
    part = whole.shape[1]
    for slot in range(4):
        at = 2 * (slot ^ spot)
        whole[at + core] = refs[slot][0:part]
        whole[at + 1 - core] = refs[4 + slot][0:part]
    split = spatial_ref.shape[0] // part
    spatial_ref[...] = whole[0:split].reshape(spatial_ref.shape)
    temporal_ref[...] = whole[split:].reshape(temporal_ref.shape)


def body(inputs, cotangent, spatial_weight, temporal_weight, norm_gain, norm_shift, spatial_bias):
    frames = lax.axis_size("frame")
    peers = lax.axis_size("chan")
    core = lax.axis_index("frame") % 2
    me = lax.axis_index("chan")
    channels, rows, cols = inputs.shape[1:]
    pixels = rows * cols
    plane, half = (channels, pixels), (channels, pixels // 2)
    tied = lax.optimization_barrier
    at = lax.axis_index("frame")
    place = jnp.stack([me, core, me // 2, (at // 2 % 2) ^ core]).astype(jnp.int32)
    table = jnp.concatenate([v[None] for v in (norm_gain, norm_shift, spatial_bias)])
    raw_in, raw_grad = inputs[0], cotangent[0]
    cross = lambda v: lax.ppermute(v, "frame", neighbour(frames))
    mate = lambda v: lax.ppermute(v, "frame", partner(1, frames))

    def meet(v, frame_bits, chan_bits):
        return lax.ppermute(v, ("frame", "chan"), both(frame_bits, chan_bits, frames, peers))

    def total(v, steps):
        got = [v] + [meet(v, *step) for step in steps]
        return got[0] + got[1] if len(got) == 2 else (got[0] + got[1]) + (got[2] + got[3])

    turned, payload = call(
        sums_kernel, [(plane, BF16), ((peers, 8 + rows, channels), F32)], [place, raw_in], cost=(0, 2 * MIB), limit=8
    )
    payload, later_grad, table = tied((payload, raw_grad, table))
    received = lax.all_to_all(payload, "chan", 0, 0, tiled=True)
    early_grad, late_grad = call(turn_kernel, [(half, BF16)] * 2, [later_grad], cost=(0, 1000), limit=8)
    crossed = [cross(early_grad)]
    received, early_grad, late_grad = tied((received, early_grad, late_grad))
    grads = [early_grad, late_grad]
    crossed.append(cross(late_grad))
    mates = [mate(v) for v in grads]

    padded = (3 * channels, pixels + 2 * cols)
    act, hidden, slope, columns = call(
        forward_kernel,
        [(padded, BF16), (plane, BF16), (plane, F32), ((channels, LANES), F32)],
        [place, turned, received, table, spatial_weight],
        cost=(1000, MIB),
        limit=16,
    )
    early_shape, late_shape = (3 * channels, channels), (3 * channels, 3 * channels)
    shifted = pltpu.VMEM((channels, pixels // 2 + 4 * cols), BF16)
    pre_early, *sums = call(
        functools.partial(backward_kernel, False),
        [(half, BF16), (early_shape, F32), (late_shape, F32), ((LANES, channels), F32)],
        [place, act, hidden, slope, grads[0], mates[0], crossed[0], temporal_weight],
        [shifted],
        cost=(1000, MIB),
        limit=20,
    )
    part = 12 * channels // 8
    slots = ((4, part, channels), F32)
    pre_late, keep, send, edges = call(
        functools.partial(backward_kernel, True),
        [(half, BF16), slots, slots, ((2 * rows, channels), F32)],
        [place, act, hidden, slope, grads[1], mates[1], crossed[1], temporal_weight, *sums],
        [pltpu.VMEM(early_shape, F32), pltpu.VMEM(late_shape, F32), shifted],
        cost=(1000, MIB),
        limit=20,
    )
    near = meet(edges, 0, 1)
    terms = keep + mate(send)
    terms, near, hidden = tied((terms, near, hidden))
    hidden_inside, hidden_mate = lax.ppermute(hidden, "frame", crossing(frames, True)), mate(hidden)
    far = near[rows:]
    one, two, three = [
        meet(jnp.concatenate([terms[b], far]) if b != 2 else terms[b], 0, 2 * b) for b in (1, 2, 3)
    ]
    piece = (terms[0] + one[:part]) + (two + three[:part])
    piece, one, three, hidden_mate = tied((piece, one, three, hidden_mate))
    scaled, sums = call(
        input_kernel,
        [(plane, F32), ((8, channels), F32)],
        [place, pre_early, pre_late, near, one, three, spatial_weight, turned, columns],
        [pltpu.VMEM(padded, BF16), pltpu.VMEM((channels, pixels + 2 * cols), F32)],
        cost=(1000, MIB),
        limit=16,
    )
    piece = total(piece, [(4, 0), (8, 0), (12, 0)])
    piece, sums = tied((piece, sums))
    sums = total(sums, [(0, 1)])
    piece = total(piece, [(16, 0)])
    piece = total(piece, [(2, 0), (0, 1), (2, 1)])
    piece, hidden, hidden_inside = tied((jnp.concatenate([piece, sums]), hidden, hidden_inside))
    flat = pltpu.VMEM((rows, channels, cols), F32)
    got = [piece] + [meet(piece, 0, 2 * b) for b in (1, 2, 3)]
    hidden_outside = lax.ppermute(hidden, "frame", crossing(frames, False))
    others = [mate(v) for v in got]
    (input_grad,) = call(
        final_kernel,
        [(raw_in.shape, BF16)],
        [*got, scaled, turned, columns, raw_grad],
        [flat],
        cost=(1000, MIB),
        limit=16,
    )
    spatial_grad, temporal_grad = call(
        place_kernel,
        [((9 * channels, channels), F32), ((3 * channels, channels), F32)],
        [place, *got, *others],
        [pltpu.VMEM((8, part, channels), F32)],
        cost=(1000, MIB),
        limit=8,
    )
    hidden_outside, input_grad, spatial_grad = tied((hidden_outside, input_grad, spatial_grad))
    (output,) = call(
        output_kernel,
        [(raw_in.shape, BF16)],
        [place, hidden, hidden_mate, hidden_inside, hidden_outside, temporal_weight, raw_in],
        [flat],
        cost=(1000, MIB),
        limit=16,
    )
    square = (-1, channels, channels)
    return (output[None], input_grad[None], spatial_grad.reshape(square), temporal_grad.reshape(square))


def solution(mesh):
    banded = P("frame", None, None, "chan")
    return jax.shard_map(
        body,
        mesh=mesh,
        in_specs=(banded, banded, P(), P(), P(), P(), P()),
        out_specs=(banded, banded, P(), P()),
        check_vma=False,
    )
```

```python
import functools

import jax
import jax.numpy as jnp
from jax import lax
from jax.experimental import pallas as pl
from jax.experimental.pallas import tpu as pltpu
from jax.sharding import PartitionSpec as P

GROUPS = 32
LANES = 128
TILE = 1024
MIB = 1024 * 1024
CONTRACT_LAST = (((1,), (1,)), ((), ()))
F32, BF16 = jnp.float32, jnp.bfloat16


def partner(bits, frames):
    return [(f, f ^ bits) for f in range(frames)]


def both(frame_bits, chan_bits, frames, peers):
    return [(f * peers + c, (f ^ frame_bits) * peers + (c ^ chan_bits)) for f in range(frames) for c in range(peers)]


def crossing(frames, inside):
    return [(f, t) for f, t in neighbour(frames) if (f // 4 == t // 4) == inside]


def neighbour(frames):
    pairs = []
    for f in range(frames):
        target = f + 1 if f % 2 else f - 1
        if 0 <= target < frames:
            pairs.append((f, target))
    return pairs


def call(kernel, outs, ins, scratch=(), cost=(0, 0), limit=24, place=pltpu.VMEM):
    smem = pl.BlockSpec(memory_space=pltpu.SMEM)
    vmem = pl.BlockSpec(memory_space=pltpu.VMEM)
    is_place = lambda v: v.dtype == jnp.int32
    flops, moved = cost
    return pl.pallas_call(
        kernel,
        out_shape=[jax.ShapeDtypeStruct(s, d) for s, d in outs],
        in_specs=[smem if is_place(v) else vmem for v in ins],
        out_specs=[pl.BlockSpec(memory_space=place)] * len(outs),
        scratch_shapes=list(scratch),
        cost_estimate=pl.CostEstimate(flops=flops, bytes_accessed=moved, transcendentals=0),
        compiler_params=pltpu.CompilerParams(vmem_limit_bytes=limit * MIB),
    )(*ins)


def lane_index(shape=(LANES, LANES)):
    return lax.broadcasted_iota(jnp.int32, shape, len(shape) - 1)


def row_at(r):
    return pl.ds(pl.multiple_of(r * LANES, LANES), LANES)


def span(row, rows):
    return slice(row * LANES, (row + rows) * LANES)


def side(parts):
    return jnp.concatenate(parts, axis=1)


def tile_at(n, extra=0):
    return pl.ds(pl.multiple_of(n * TILE, LANES) + extra, TILE)


def group_sum(v):
    lane = lax.broadcasted_iota(jnp.int32, v.shape, 1)
    for step in (1, 2):
        up, down = pltpu.roll(v, LANES - step, 1), pltpu.roll(v, step, 1)
        v = v + jnp.where((lane // step) % 2 == 0, up, down)
    return v


def sigmoid(v):
    return 1.0 / (1.0 + jnp.exp(-v))


def selector(n, rows):
    pixel = lax.broadcasted_iota(jnp.int32, (LANES, TILE), 1) + n * TILE
    at = lax.broadcasted_iota(jnp.int32, (LANES, TILE), 0)
    low = (at < rows) & (pixel == at * LANES)
    high = (at >= 64) & (pixel == (at - 64) * LANES + (LANES - 1))
    return jnp.where(low | high | (at == 32), 1.0, 0.0).astype(BF16)


def turn(raw):
    return jnp.swapaxes(raw, 0, 1)


def store_shifts(ref, row, halo, r, lane, order, offset=1):
    row = row.astype(BF16)
    left = jnp.where(lane == 0, pltpu.roll(halo, LANES - 32 - r, 1), pltpu.roll(row, 1, 1))
    right = jnp.where(lane == LANES - 1, pltpu.roll(halo, 63 - r, 1), pltpu.roll(row, LANES - 1, 1))
    shifts = (left, row, right)
    for slot, which in enumerate(order):
        ref[slot * LANES : (slot + 1) * LANES, row_at(r + offset)] = shifts[which].astype(BF16)


def turn_kernel(raw_ref, low_ref, high_ref):
    channels, rows, _ = raw_ref.shape
    for c in range(0, channels, 16):
        block = turn(raw_ref[c : c + 16])
        for r in range(rows):
            ref, at = (low_ref, r) if r < rows // 2 else (high_ref, r - rows // 2)
            ref[c : c + 16, at * LANES : (at + 1) * LANES] = block[r]


def sums_kernel(me_ref, raw_ref, out_ref, payload_ref):
    channels, rows, _ = raw_ref.shape
    me = me_ref[0]
    for c in range(0, channels, 16):
        block = turn(raw_ref[c : c + 16])
        for r in range(rows):
            out_ref[c : c + 16, r * LANES : (r + 1) * LANES] = block[r]
    packed = jnp.zeros((LANES, channels), F32)
    for n in range(rows * LANES // TILE):
        packed += lax.dot_general(selector(n, rows), out_ref[:, n * TILE : (n + 1) * TILE], CONTRACT_LAST, preferred_element_type=F32)
    mean = packed[32:33] / (rows * LANES)
    mean_all = jnp.broadcast_to(mean, (LANES, channels)).T

    def square(r, acc):
        off = out_ref[:, row_at(r)].astype(F32) - mean_all
        return acc + off * off

    squares = lax.fori_loop(0, rows, square, jnp.zeros((channels, LANES), F32), unroll=4)
    squares = jnp.sum(squares.T, axis=0, keepdims=True)
    head = jnp.concatenate([mean, squares, jnp.zeros((6, channels), F32)], axis=0)
    for peer in range(payload_ref.shape[0]):
        payload_ref[peer, 0:8, :] = head
        payload_ref[peer, 8 : 8 + rows, :] = jnp.where(peer < me, packed[0:rows], packed[64 : 64 + rows])


def forward_kernel(me_ref, plane_ref, received_ref, table_ref, weight_ref, act_ref, hidden_ref, slope_ref, columns_ref):
    channels, pixels = plane_ref.shape
    rows = pixels // LANES
    peers = received_ref.shape[0]
    me = me_ref[0]
    lane = lane_index()
    count = (channels // GROUPS) * pixels * peers
    means, squares = received_ref[:, 0, :], received_ref[:, 1, :]
    center = group_sum(jnp.sum(means, axis=0, keepdims=True)) * (GROUPS / (channels * peers))
    off = means - center
    spread = group_sum(jnp.sum(squares + pixels * (off * off), axis=0, keepdims=True)) / count
    inverse = lax.rsqrt(spread + 1e-05)
    low = received_ref[jnp.maximum(me - 1, 0), 8 : 8 + rows, :]
    high = received_ref[jnp.minimum(me + 1, peers - 1), 8 : 8 + rows, :]
    head = jnp.concatenate([center, inverse, table_ref[...], jnp.zeros((3, LANES), F32)], axis=0)
    gap = jnp.zeros((24, LANES), F32)
    columns = jnp.concatenate([head, gap, low, high, jnp.zeros((32, LANES), F32)], axis=0).T
    columns_ref[...] = columns
    wide = lambda at: jnp.broadcast_to(columns[:, at : at + 1], (channels, LANES))
    center_w, inverse_w, gain_w, shift_w, bias_w = [wide(at) for at in range(5)]

    def activate(v):
        v = (v - center_w) * inverse_w * gain_w + shift_w
        return v * sigmoid(v)

    inside = ((lane < 64) & (me > 0)) | ((lane >= 64) & (me < peers - 1))
    halo = jnp.where(inside, activate(columns), 0.0).astype(BF16)
    nothing = jnp.zeros((3 * channels, LANES), BF16)
    act_ref[:, 0:LANES] = nothing
    act_ref[:, (rows + 1) * LANES : (rows + 2) * LANES] = nothing

    def shape_row(r, carry):
        row = activate(plane_ref[:, row_at(r)].astype(F32))
        store_shifts(act_ref, row, halo, r, lane, (0, 1, 2))
        return carry

    lax.fori_loop(0, rows, shape_row, 0, unroll=8)
    weights = side([weight_ref[t] for t in range(9)])
    each = TILE // LANES
    bias = jnp.broadcast_to(bias_w[:, 0:1], (channels, TILE))
    for n in range(rows // each):
        window = jnp.concatenate([act_ref[:, span(n * each + dy, each)] for dy in range(3)], axis=0)
        value = jnp.dot(weights, window, preferred_element_type=F32) + bias
        logistic = sigmoid(value)
        hidden_ref[:, span(n * each, each)] = (value * logistic).astype(BF16)
        slope_ref[:, span(n * each, each)] = logistic * (1.0 + value * (1.0 - logistic))


def backward_kernel(last, me_ref, act_ref, hidden_ref, slope_ref, grad_ref, mate_ref, cross_ref, *rest):
    if last:
        weight_ref, early_in, late_in, packed_in, *rest = rest
        pre_ref, keep_ref, send_ref, edges_ref, early, late, shifted = rest
    else:
        weight_ref, pre_ref, early, late, packed_ref, shifted = rest
    channels, pixels = grad_ref.shape
    rows = 2 * pixels // LANES
    core, spot = me_ref[1], me_ref[2]
    turned = [weight_ref[k].astype(F32).T for k in range(3)]
    even = core == 0
    ahead = jnp.where(even, turned[0], turned[2])
    behind = jnp.where(even, turned[2], turned[0])
    weights = jnp.concatenate([turned[1], ahead, behind], axis=1).astype(BF16)
    own_rows = rows // 2
    start = own_rows if last else 0
    blank = jnp.zeros((channels, 2 * LANES), BF16)
    shifted[:, span(0, 2)] = blank
    shifted[:, span(own_rows + 2, 2)] = blank
    each = TILE // LANES
    fresh = jnp.zeros((3 * channels, channels), F32)
    packed = jnp.zeros((LANES, channels), F32)
    for n in range(own_rows // each):
        at, whole = span(n * each, each), span(n * each + start, each)
        grads = jnp.concatenate([ref[:, at] for ref in (grad_ref, mate_ref, cross_ref)], axis=0)
        back = jnp.dot(weights, grads, preferred_element_type=F32)
        pre = (back * slope_ref[:, whole]).astype(BF16)
        pre_ref[:, at] = pre
        shifted[:, span(n * each + 2, each)] = pre
        fresh += lax.dot_general(grads, hidden_ref[:, whole], CONTRACT_LAST, preferred_element_type=F32)
        packed += lax.dot_general(selector(n + start // each, rows), pre, CONTRACT_LAST, preferred_element_type=F32)
    lhs = jnp.concatenate([shifted[:, span(2 - dy, own_rows + 2)] for dy in range(3)], axis=0)
    rhs = act_ref[:, span(start, own_rows + 2)]
    latest = lax.dot_general(lhs, rhs, CONTRACT_LAST, preferred_element_type=F32)
    early[...] = fresh + early_in[...] if last else fresh
    late[...] = latest + late_in[...] if last else latest
    packed = packed + packed_in[...] if last else packed
    if not last:
        packed_ref[...] = packed
        return
    low, high = packed[0:rows], packed[64 : 64 + rows]
    left = me_ref[0] % 2 == 0
    edges_ref[0:rows, :] = jnp.where(left, high, low)
    edges_ref[rows:, :] = jnp.where(left, low, high)
    own, mate, cross = [early[i * channels : (i + 1) * channels, :] for i in range(3)]
    blocks = [late[t // 3 * channels : (t // 3 + 1) * channels, span(t % 3, 1)] for t in range(9)]
    blocks += [jnp.where(even, mate, cross), own, jnp.where(even, cross, mate)]
    part = keep_ref.shape[1]

    def rows_at(at):
        return blocks[at // channels][at % channels : at % channels + 64]

    for y in range(4):
        slot = y ^ spot
        for v in range(0, part, 64):
            one, two = rows_at(2 * y * part + v), rows_at((2 * y + 1) * part + v)
            keep_ref[slot, v : v + 64, :] = jnp.where(even, one, two)
            send_ref[slot, v : v + 64, :] = jnp.where(even, two, one)


def input_kernel(me_ref, early_ref, late_ref, near_ref, one_ref, three_ref, *refs):
    weight_ref, plane_ref, columns_ref, scaled_ref, sums_ref, padded, total = refs
    channels, pixels = plane_ref.shape
    rows = pixels // LANES
    lane = lane_index()
    blank = jnp.zeros((32, LANES), F32)
    me = me_ref[0]
    left = me % 2 == 0
    near = near_ref[0:rows, :]
    at = one_ref.shape[0] - rows
    far = jnp.where((me // 2 % 2 == 0) != left, one_ref[at:, :], three_ref[at:, :])
    far = jnp.where((me > 0) & (me < 7), far, 0.0)
    low, high = jnp.where(left, far, near), jnp.where(left, near, far)
    halo = jnp.concatenate([blank, low, high, blank], axis=0).T.astype(BF16)
    for first, ref in ((0, early_ref), (rows // 2, late_ref)):

        def shift_row(r, carry, ref=ref, first=first):
            store_shifts(padded, ref[:, row_at(r)], halo, r + first, lane, (2, 1, 0))
            return carry

        lax.fori_loop(0, rows // 2, shift_row, 0, unroll=8)
    flipped = lambda t: weight_ref[t].astype(F32).T.astype(BF16)
    weights = side([flipped(3 * dy + dx) for dy in (2, 1, 0) for dx in range(3)])
    each = TILE // LANES
    padded[:, span(0, 1)] = jnp.zeros((3 * channels, LANES), BF16)
    padded[:, span(rows + 1, 1)] = jnp.zeros((3 * channels, LANES), BF16)
    for n in range(rows // each):
        window = jnp.concatenate([padded[:, span(n * each + dy, each)] for dy in range(3)], axis=0)
        total[:, span(n * each + 1, each)] = jnp.dot(weights, window, preferred_element_type=F32)
    columns = columns_ref[...]
    wide = lambda at: jnp.broadcast_to(columns[:, at : at + 1], (channels, LANES))
    center, inverse, gain, shift = [wide(at) for at in range(4)]

    def step(r, carry):
        plain, crossed = carry
        normed = (plane_ref[:, row_at(r)].astype(F32) - center) * inverse
        shaped = normed * gain + shift
        logistic = sigmoid(shaped)
        scaled = total[:, row_at(r + 1)] * (logistic * (1.0 + shaped * (1.0 - logistic))) * gain
        scaled_ref[:, row_at(r)] = scaled
        return plain + scaled, crossed + scaled * normed

    zero = jnp.zeros((channels, LANES), F32)
    plain, crossed = lax.fori_loop(0, rows, step, (zero, zero), unroll=4)
    plain, crossed = [jnp.sum(v, axis=1, keepdims=True) for v in (plain, crossed)]
    sums_ref[...] = jnp.where(lane == 0, plain, jnp.where(lane == 1, crossed, 0.0)).T[0:8]


def partial_kernel(me_ref, hidden_ref, mate_ref, inside_ref, weight_ref, raw_ref, out_ref, flat):
    channels, rows, _ = raw_ref.shape
    even = me_ref[1] == 0
    pick = lambda a, b: jnp.where(even, weight_ref[a].astype(F32), weight_ref[b].astype(F32)).astype(BF16)
    weights = jnp.concatenate([weight_ref[1], pick(2, 0), pick(0, 2)], axis=1)
    each = TILE // LANES
    for n in range(rows // each):
        at = span(n * each, each)
        frames = jnp.concatenate([ref[:, at] for ref in (hidden_ref, mate_ref, inside_ref)], axis=0)
        mixed = jnp.dot(weights, frames, preferred_element_type=F32)
        for i in range(each):
            flat[n * each + i] = mixed[:, span(i, 1)]
    for c in range(0, channels, 16):
        out_ref[c : c + 16] = raw_ref[c : c + 16].astype(F32) + turn(flat[:, c : c + 16, :])


def close_kernel(me_ref, *refs):
    partial_ref, outside_ref, weight_ref, spatial_ref, temporal_ref, out_ref, whole, flat, staged, sems = refs[8:]
    core, spot = me_ref[1], me_ref[2]
    channels, rows, _ = partial_ref.shape
    part = whole.shape[1]
    for slot in range(4):
        at = 2 * (slot ^ spot)
        whole[at + core] = refs[slot][0:part]
        whole[at + 1 - core] = refs[4 + slot][0:part]
    split, blocks = spatial_ref.shape[0], channels // 16
    copies = [
        pltpu.make_async_copy(whole.at[0:split], spatial_ref, sems.at[blocks]),
        pltpu.make_async_copy(whole.at[split:], temporal_ref, sems.at[blocks + 1]),
    ]
    for copy in copies:
        copy.start()
    weight = jnp.where(core == 0, weight_ref[0].astype(F32), weight_ref[2].astype(F32)).astype(BF16)
    each = TILE // LANES
    for n in range(rows // each):
        mixed = jnp.dot(weight, outside_ref[:, span(n * each, each)], preferred_element_type=F32)
        for i in range(each):
            flat[n * each + i] = mixed[:, span(i, 1)]
    for i in range(blocks):
        at = slice(16 * i, 16 * i + 16)
        staged[at] = (partial_ref[at] + turn(flat[:, at, :])).astype(BF16)
        copies.append(pltpu.make_async_copy(staged.at[at], out_ref.at[at], sems.at[i]))
        copies[-1].start()
    for copy in copies:
        copy.wait()


def final_kernel(own_ref, one_ref, two_ref, three_ref, scaled_ref, plane_ref, columns_ref, raw_ref, out_ref, flat, staged, sems):
    channels, rows, _ = raw_ref.shape
    count = (channels // GROUPS) * rows * LANES * 8
    at = own_ref.shape[0] - 8
    totals = (own_ref[at:, :] + one_ref[at:, :]) + (two_ref[at:, :] + three_ref[at:, :])
    totals = group_sum(totals) / count
    turned = jnp.concatenate([totals, jnp.zeros((LANES - 8, LANES), F32)], axis=0).T
    wide = lambda v, at: jnp.broadcast_to(v[:, at : at + 1], (channels, LANES))
    mean_grad, second = wide(turned, 0), wide(turned, 1)
    columns = columns_ref[...]
    center, inverse = wide(columns, 0), wide(columns, 1)

    def step(r, carry):
        normed = (plane_ref[:, row_at(r)].astype(F32) - center) * inverse
        flat[r] = inverse * (scaled_ref[:, row_at(r)] - mean_grad - normed * second)
        return carry

    lax.fori_loop(0, rows, step, 0, unroll=2)
    copies = []
    for i in range(channels // 16):
        at = slice(16 * i, 16 * i + 16)
        staged[at] = (raw_ref[at].astype(F32) + turn(flat[:, at, :])).astype(BF16)
        copies.append(pltpu.make_async_copy(staged.at[at], out_ref.at[at], sems.at[i]))
        copies[-1].start()
    for copy in copies:
        copy.wait()


def body(inputs, cotangent, spatial_weight, temporal_weight, norm_gain, norm_shift, spatial_bias):
    frames = lax.axis_size("frame")
    peers = lax.axis_size("chan")
    core = lax.axis_index("frame") % 2
    me = lax.axis_index("chan")
    channels, rows, cols = inputs.shape[1:]
    pixels = rows * cols
    plane, half = (channels, pixels), (channels, pixels // 2)
    tied = lax.optimization_barrier
    at = lax.axis_index("frame")
    place = jnp.stack([me, core, me // 2, (at // 2 % 2) ^ core]).astype(jnp.int32)
    table = jnp.concatenate([v[None] for v in (norm_gain, norm_shift, spatial_bias)])
    place, table = tied((place, table))
    raw_in, raw_grad = inputs[0], cotangent[0]
    cross = lambda v: lax.ppermute(v, "frame", neighbour(frames))
    mate = lambda v: lax.ppermute(v, "frame", partner(1, frames))

    def meet(v, frame_bits, chan_bits):
        return lax.ppermute(v, ("frame", "chan"), both(frame_bits, chan_bits, frames, peers))

    def total(v, steps):
        got = [v] + [meet(v, *step) for step in steps]
        return got[0] + got[1] if len(got) == 2 else (got[0] + got[1]) + (got[2] + got[3])

    turned, payload = call(
        sums_kernel, [(plane, BF16), ((peers, 8 + rows, channels), F32)], [place, raw_in], cost=(0, 2 * MIB), limit=8
    )
    payload, later_grad = tied((payload, raw_grad))
    received = lax.all_to_all(payload, "chan", 0, 0, tiled=True)
    early_grad, late_grad = call(turn_kernel, [(half, BF16)] * 2, [later_grad], cost=(0, 1000), limit=8)
    crossed = [cross(early_grad)]
    received, early_grad, late_grad = tied((received, early_grad, late_grad))
    grads = [early_grad, late_grad]
    crossed.append(cross(late_grad))
    mates = [mate(v) for v in grads]

    padded = (3 * channels, pixels + 2 * cols)
    act, hidden, slope, columns = call(
        forward_kernel,
        [(padded, BF16), (plane, BF16), (plane, F32), ((channels, LANES), F32)],
        [place, turned, received, table, spatial_weight],
        cost=(1000, MIB),
        limit=16,
    )
    early_shape, late_shape = (3 * channels, channels), (3 * channels, 3 * channels)
    shifted = pltpu.VMEM((channels, pixels // 2 + 4 * cols), BF16)
    pre_early, *sums = call(
        functools.partial(backward_kernel, False),
        [(half, BF16), (early_shape, F32), (late_shape, F32), ((LANES, channels), F32)],
        [place, act, hidden, slope, grads[0], mates[0], crossed[0], temporal_weight],
        [shifted],
        cost=(1000, MIB),
        limit=20,
    )
    part = 12 * channels // 8
    slots = ((4, part, channels), F32)
    pre_late, keep, send, edges = call(
        functools.partial(backward_kernel, True),
        [(half, BF16), slots, slots, ((2 * rows, channels), F32)],
        [place, act, hidden, slope, grads[1], mates[1], crossed[1], temporal_weight, *sums],
        [pltpu.VMEM(early_shape, F32), pltpu.VMEM(late_shape, F32), shifted],
        cost=(1000, MIB),
        limit=20,
    )
    near = meet(edges, 0, 1)
    terms = keep + mate(send)
    terms, near, hidden = tied((terms, near, hidden))
    hidden_inside, hidden_mate = lax.ppermute(hidden, "frame", crossing(frames, True)), mate(hidden)
    far = near[rows:]
    one, two, three = [
        meet(jnp.concatenate([terms[b], far]) if b != 2 else terms[b], 0, 2 * b) for b in (1, 2, 3)
    ]
    piece = (terms[0] + one[:part]) + (two + three[:part])
    piece, one, three, hidden_mate = tied((piece, one, three, hidden_mate))
    scaled, sums = call(
        input_kernel,
        [(plane, F32), ((8, channels), F32)],
        [place, pre_early, pre_late, near, one, three, spatial_weight, turned, columns],
        [pltpu.VMEM(padded, BF16), pltpu.VMEM((channels, pixels + 2 * cols), F32)],
        cost=(1000, MIB),
        limit=16,
    )
    piece = total(piece, [(4, 0), (8, 0), (12, 0)])
    piece, sums = tied((piece, sums))
    piece = total(piece, [(28, 0)])
    both_x = total(jnp.concatenate([piece, sums]), [(0, 1)])
    both_x, hidden_inside = tied((both_x, hidden_inside))
    piece, sums = both_x[:part], both_x[part:]
    flat = pltpu.VMEM((rows, channels, cols), F32)
    (partial,) = call(
        partial_kernel,
        [(raw_in.shape, F32)],
        [place, hidden, hidden_mate, hidden_inside, temporal_weight, raw_in],
        [flat],
        cost=(1, 1),
        limit=16,
    )
    piece = total(piece, [(2, 1)])
    piece, hidden, partial = tied((jnp.concatenate([piece, sums]), hidden, partial))
    got = [piece] + [meet(piece, 0, 2 * b) for b in (1, 2, 3)]
    hidden_outside = lax.ppermute(hidden, "frame", crossing(frames, False))
    others = [mate(v) for v in got]
    staged, sems = pltpu.VMEM(raw_in.shape, BF16), pltpu.SemaphoreType.DMA((10,))
    (input_grad,) = call(
        final_kernel,
        [(raw_in.shape, BF16)],
        [*got, scaled, turned, columns, raw_grad],
        [flat, staged, sems],
        cost=(1000, MIB),
        limit=16,
        place=pl.ANY,
    )
    hidden_outside, input_grad = tied((hidden_outside, input_grad))
    spatial_grad, temporal_grad, output = call(
        close_kernel,
        [((6, part, channels), F32), ((2, part, channels), F32), (raw_in.shape, BF16)],
        [place, *got, *others, partial, hidden_outside, temporal_weight],
        [pltpu.VMEM((8, part, channels), F32), flat, staged, sems],
        cost=(1000, MIB),
        limit=16,
        place=pl.ANY,
    )
    square = (-1, channels, channels)
    return (output[None], input_grad[None], spatial_grad.reshape(square), temporal_grad.reshape(square))


def solution(mesh):
    banded = P("frame", None, None, "chan")
    return jax.shard_map(
        body,
        mesh=mesh,
        in_specs=(banded, banded, P(), P(), P(), P(), P()),
        out_specs=(banded, banded, P(), P()),
        check_vma=False,
    )
```

```python
import functools

import jax
import jax.numpy as jnp
from jax import lax
from jax.experimental import pallas as pl
from jax.experimental.pallas import tpu as pltpu
from jax.sharding import PartitionSpec as P

GROUPS = 32
LANES = 128
TILE = 1024
MIB = 1024 * 1024
CONTRACT_LAST = (((1,), (1,)), ((), ()))
F32, BF16 = jnp.float32, jnp.bfloat16


def partner(bits, frames):
    return [(f, f ^ bits) for f in range(frames)]


def both(frame_bits, chan_bits, frames, peers):
    return [(f * peers + c, (f ^ frame_bits) * peers + (c ^ chan_bits)) for f in range(frames) for c in range(peers)]


def crossing(frames, inside):
    return [(f, t) for f, t in neighbour(frames) if (f // 4 == t // 4) == inside]


def neighbour(frames):
    pairs = []
    for f in range(frames):
        target = f + 1 if f % 2 else f - 1
        if 0 <= target < frames:
            pairs.append((f, target))
    return pairs


def call(kernel, outs, ins, scratch=(), cost=(0, 0), limit=24, place=pltpu.VMEM):
    smem = pl.BlockSpec(memory_space=pltpu.SMEM)
    vmem = pl.BlockSpec(memory_space=pltpu.VMEM)
    is_place = lambda v: v.dtype == jnp.int32
    flops, moved = cost
    return pl.pallas_call(
        kernel,
        out_shape=[jax.ShapeDtypeStruct(s, d) for s, d in outs],
        in_specs=[smem if is_place(v) else vmem for v in ins],
        out_specs=[pl.BlockSpec(memory_space=place)] * len(outs),
        scratch_shapes=list(scratch),
        cost_estimate=pl.CostEstimate(flops=flops, bytes_accessed=moved, transcendentals=0),
        compiler_params=pltpu.CompilerParams(vmem_limit_bytes=limit * MIB),
    )(*ins)


def lane_index(shape=(LANES, LANES)):
    return lax.broadcasted_iota(jnp.int32, shape, len(shape) - 1)


def row_at(r):
    return pl.ds(pl.multiple_of(r * LANES, LANES), LANES)


def span(row, rows):
    return slice(row * LANES, (row + rows) * LANES)


def side(parts):
    return jnp.concatenate(parts, axis=1)


def tile_at(n, extra=0):
    return pl.ds(pl.multiple_of(n * TILE, LANES) + extra, TILE)


def group_sum(v):
    lane = lax.broadcasted_iota(jnp.int32, v.shape, 1)
    for step in (1, 2):
        up, down = pltpu.roll(v, LANES - step, 1), pltpu.roll(v, step, 1)
        v = v + jnp.where((lane // step) % 2 == 0, up, down)
    return v


def sigmoid(v):
    return 1.0 / (1.0 + jnp.exp(-v))


def selector(n, rows):
    pixel = lax.broadcasted_iota(jnp.int32, (LANES, TILE), 1) + n * TILE
    at = lax.broadcasted_iota(jnp.int32, (LANES, TILE), 0)
    low = (at < rows) & (pixel == at * LANES)
    high = (at >= 64) & (pixel == (at - 64) * LANES + (LANES - 1))
    return jnp.where(low | high | (at == 32), 1.0, 0.0).astype(BF16)


def turn(raw):
    return jnp.swapaxes(raw, 0, 1)


def store_shifts(ref, row, halo, r, lane, order, offset=1):
    row = row.astype(BF16)
    left = jnp.where(lane == 0, pltpu.roll(halo, LANES - 32 - r, 1), pltpu.roll(row, 1, 1))
    right = jnp.where(lane == LANES - 1, pltpu.roll(halo, 63 - r, 1), pltpu.roll(row, LANES - 1, 1))
    shifts = (left, row, right)
    for slot, which in enumerate(order):
        ref[slot * LANES : (slot + 1) * LANES, row_at(r + offset)] = shifts[which].astype(BF16)


def turn_kernel(raw_ref, low_ref, high_ref):
    channels, rows, _ = raw_ref.shape
    for c in range(0, channels, 16):
        block = turn(raw_ref[c : c + 16])
        for r in range(rows):
            ref, at = (low_ref, r) if r < rows // 2 else (high_ref, r - rows // 2)
            ref[c : c + 16, at * LANES : (at + 1) * LANES] = block[r]


def sums_kernel(me_ref, raw_ref, out_ref, payload_ref):
    channels, rows, _ = raw_ref.shape
    me = me_ref[0]
    for c in range(0, channels, 16):
        block = turn(raw_ref[c : c + 16])
        for r in range(rows):
            out_ref[c : c + 16, r * LANES : (r + 1) * LANES] = block[r]
    packed = jnp.zeros((LANES, channels), F32)
    for n in range(rows * LANES // TILE):
        packed += lax.dot_general(selector(n, rows), out_ref[:, n * TILE : (n + 1) * TILE], CONTRACT_LAST, preferred_element_type=F32)
    mean = packed[32:33] / (rows * LANES)
    mean_all = jnp.broadcast_to(mean, (LANES, channels)).T

    def square(r, acc):
        off = out_ref[:, row_at(r)].astype(F32) - mean_all
        return acc + off * off

    squares = lax.fori_loop(0, rows, square, jnp.zeros((channels, LANES), F32), unroll=4)
    squares = jnp.sum(squares.T, axis=0, keepdims=True)
    head = jnp.concatenate([mean, squares, jnp.zeros((6, channels), F32)], axis=0)
    for peer in range(payload_ref.shape[0]):
        payload_ref[peer, 0:8, :] = head
        payload_ref[peer, 8 : 8 + rows, :] = jnp.where(peer < me, packed[0:rows], packed[64 : 64 + rows])


def forward_kernel(me_ref, plane_ref, received_ref, table_ref, weight_ref, act_ref, hidden_ref, slope_ref, columns_ref):
    channels, pixels = plane_ref.shape
    rows = pixels // LANES
    peers = received_ref.shape[0]
    me = me_ref[0]
    lane = lane_index()
    count = (channels // GROUPS) * pixels * peers
    means, squares = received_ref[:, 0, :], received_ref[:, 1, :]
    center = group_sum(jnp.sum(means, axis=0, keepdims=True)) * (GROUPS / (channels * peers))
    off = means - center
    spread = group_sum(jnp.sum(squares + pixels * (off * off), axis=0, keepdims=True)) / count
    inverse = lax.rsqrt(spread + 1e-05)
    low = received_ref[jnp.maximum(me - 1, 0), 8 : 8 + rows, :]
    high = received_ref[jnp.minimum(me + 1, peers - 1), 8 : 8 + rows, :]
    head = jnp.concatenate([center, inverse, table_ref[...], jnp.zeros((3, LANES), F32)], axis=0)
    gap = jnp.zeros((24, LANES), F32)
    columns = jnp.concatenate([head, gap, low, high, jnp.zeros((32, LANES), F32)], axis=0).T
    columns_ref[...] = columns
    wide = lambda at: jnp.broadcast_to(columns[:, at : at + 1], (channels, LANES))
    center_w, inverse_w, gain_w, shift_w, bias_w = [wide(at) for at in range(5)]

    def activate(v):
        v = (v - center_w) * inverse_w * gain_w + shift_w
        return v * sigmoid(v)

    inside = ((lane < 64) & (me > 0)) | ((lane >= 64) & (me < peers - 1))
    halo = jnp.where(inside, activate(columns), 0.0).astype(BF16)
    nothing = jnp.zeros((3 * channels, LANES), BF16)
    act_ref[:, 0:LANES] = nothing
    act_ref[:, (rows + 1) * LANES : (rows + 2) * LANES] = nothing

    def shape_row(r, carry):
        row = activate(plane_ref[:, row_at(r)].astype(F32))
        store_shifts(act_ref, row, halo, r, lane, (0, 1, 2))
        return carry

    lax.fori_loop(0, rows, shape_row, 0, unroll=8)
    weights = side([weight_ref[t] for t in range(9)])
    each = TILE // LANES
    bias = jnp.broadcast_to(bias_w[:, 0:1], (channels, TILE))
    for n in range(rows // each):
        window = jnp.concatenate([act_ref[:, span(n * each + dy, each)] for dy in range(3)], axis=0)
        value = jnp.dot(weights, window, preferred_element_type=F32) + bias
        logistic = sigmoid(value)
        hidden_ref[:, span(n * each, each)] = (value * logistic).astype(BF16)
        slope_ref[:, span(n * each, each)] = logistic * (1.0 + value * (1.0 - logistic))


def backward_kernel(last, me_ref, act_ref, hidden_ref, slope_ref, grad_ref, mate_ref, cross_ref, *rest):
    if last:
        inside_ref, weight_ref, early_in, late_in, packed_in, *rest = rest
        inside = me_ref[3] == 1
        pre_ref, keep_ref, send_ref, edges_ref, early, late, shifted = rest
    else:
        weight_ref, pre_ref, early, late, packed_ref, shifted = rest
    channels, pixels = grad_ref.shape
    rows = 2 * pixels // LANES
    core, spot = me_ref[1], me_ref[2]
    turned = [weight_ref[k].astype(F32).T for k in range(3)]
    even = core == 0
    ahead = jnp.where(even, turned[0], turned[2])
    behind = jnp.where(even, turned[2], turned[0])
    weights = jnp.concatenate([turned[1], ahead, behind], axis=1).astype(BF16)
    own_rows = rows // 2
    start = own_rows if last else 0
    blank = jnp.zeros((channels, 2 * LANES), BF16)
    shifted[:, span(0, 2)] = blank
    shifted[:, span(own_rows + 2, 2)] = blank
    each = TILE // LANES
    fresh = jnp.zeros((3 * channels, channels), F32)
    packed = jnp.zeros((LANES, channels), F32)
    for n in range(own_rows // each):
        at, whole = span(n * each, each), span(n * each + start, each)
        across = cross_ref[:, at]
        if last:
            across = jnp.where(inside, inside_ref[:, at], across)
        grads = jnp.concatenate([grad_ref[:, at], mate_ref[:, at], across], axis=0)
        back = jnp.dot(weights, grads, preferred_element_type=F32)
        pre = (back * slope_ref[:, whole]).astype(BF16)
        pre_ref[:, at] = pre
        shifted[:, span(n * each + 2, each)] = pre
        fresh += lax.dot_general(grads, hidden_ref[:, whole], CONTRACT_LAST, preferred_element_type=F32)
        packed += lax.dot_general(selector(n + start // each, rows), pre, CONTRACT_LAST, preferred_element_type=F32)
    lhs = jnp.concatenate([shifted[:, span(2 - dy, own_rows + 2)] for dy in range(3)], axis=0)
    rhs = act_ref[:, span(start, own_rows + 2)]
    latest = lax.dot_general(lhs, rhs, CONTRACT_LAST, preferred_element_type=F32)
    early[...] = fresh + early_in[...] if last else fresh
    late[...] = latest + late_in[...] if last else latest
    packed = packed + packed_in[...] if last else packed
    if not last:
        packed_ref[...] = packed
        return
    low, high = packed[0:rows], packed[64 : 64 + rows]
    left = me_ref[0] % 2 == 0
    edges_ref[0:rows, :] = jnp.where(left, high, low)
    edges_ref[rows:, :] = jnp.where(left, low, high)
    own, mate, cross = [early[i * channels : (i + 1) * channels, :] for i in range(3)]
    blocks = [late[t // 3 * channels : (t // 3 + 1) * channels, span(t % 3, 1)] for t in range(9)]
    blocks += [jnp.where(even, mate, cross), own, jnp.where(even, cross, mate)]
    part = keep_ref.shape[1]

    def rows_at(at):
        return blocks[at // channels][at % channels : at % channels + 64]

    for y in range(4):
        slot = y ^ spot
        for v in range(0, part, 64):
            one, two = rows_at(2 * y * part + v), rows_at((2 * y + 1) * part + v)
            keep_ref[slot, v : v + 64, :] = jnp.where(even, one, two)
            send_ref[slot, v : v + 64, :] = jnp.where(even, two, one)


def input_kernel(me_ref, early_ref, late_ref, near_ref, one_ref, three_ref, *refs):
    weight_ref, plane_ref, columns_ref, scaled_ref, sums_ref, padded, total = refs
    channels, pixels = plane_ref.shape
    rows = pixels // LANES
    lane = lane_index()
    blank = jnp.zeros((32, LANES), F32)
    me = me_ref[0]
    left = me % 2 == 0
    near = near_ref[0:rows, :]
    at = one_ref.shape[0] - rows
    far = jnp.where((me // 2 % 2 == 0) != left, one_ref[at:, :], three_ref[at:, :])
    far = jnp.where((me > 0) & (me < 7), far, 0.0)
    low, high = jnp.where(left, far, near), jnp.where(left, near, far)
    halo = jnp.concatenate([blank, low, high, blank], axis=0).T.astype(BF16)
    for first, ref in ((0, early_ref), (rows // 2, late_ref)):

        def shift_row(r, carry, ref=ref, first=first):
            store_shifts(padded, ref[:, row_at(r)], halo, r + first, lane, (2, 1, 0))
            return carry

        lax.fori_loop(0, rows // 2, shift_row, 0, unroll=8)
    flipped = lambda t: weight_ref[t].astype(F32).T.astype(BF16)
    weights = side([flipped(3 * dy + dx) for dy in (2, 1, 0) for dx in range(3)])
    each = TILE // LANES
    padded[:, span(0, 1)] = jnp.zeros((3 * channels, LANES), BF16)
    padded[:, span(rows + 1, 1)] = jnp.zeros((3 * channels, LANES), BF16)
    for n in range(rows // each):
        window = jnp.concatenate([padded[:, span(n * each + dy, each)] for dy in range(3)], axis=0)
        total[:, span(n * each + 1, each)] = jnp.dot(weights, window, preferred_element_type=F32)
    columns = columns_ref[...]
    wide = lambda at: jnp.broadcast_to(columns[:, at : at + 1], (channels, LANES))
    center, inverse, gain, shift = [wide(at) for at in range(4)]

    def step(r, carry):
        plain, crossed = carry
        normed = (plane_ref[:, row_at(r)].astype(F32) - center) * inverse
        shaped = normed * gain + shift
        logistic = sigmoid(shaped)
        scaled = total[:, row_at(r + 1)] * (logistic * (1.0 + shaped * (1.0 - logistic))) * gain
        scaled_ref[:, row_at(r)] = scaled
        return plain + scaled, crossed + scaled * normed

    zero = jnp.zeros((channels, LANES), F32)
    plain, crossed = lax.fori_loop(0, rows, step, (zero, zero), unroll=4)
    plain, crossed = [jnp.sum(v, axis=1, keepdims=True) for v in (plain, crossed)]
    sums_ref[...] = jnp.where(lane == 0, plain, jnp.where(lane == 1, crossed, 0.0)).T[0:8]


def partial_kernel(me_ref, hidden_ref, mate_ref, inside_ref, weight_ref, raw_ref, out_ref, flat):
    channels, rows, _ = raw_ref.shape
    even = me_ref[1] == 0
    pick = lambda a, b: jnp.where(even, weight_ref[a].astype(F32), weight_ref[b].astype(F32)).astype(BF16)
    weights = jnp.concatenate([weight_ref[1], pick(2, 0), pick(0, 2)], axis=1)
    each = TILE // LANES
    for n in range(rows // each):
        at = span(n * each, each)
        frames = jnp.concatenate([ref[:, at] for ref in (hidden_ref, mate_ref, inside_ref)], axis=0)
        mixed = jnp.dot(weights, frames, preferred_element_type=F32)
        for i in range(each):
            flat[n * each + i] = mixed[:, span(i, 1)]
    for c in range(0, channels, 16):
        out_ref[c : c + 16] = raw_ref[c : c + 16].astype(F32) + turn(flat[:, c : c + 16, :])


def close_kernel(me_ref, *refs):
    partial_ref, outside_ref, weight_ref, spatial_ref, temporal_ref, out_ref, whole, flat, staged, sems = refs[8:]
    core, spot = me_ref[1], me_ref[2]
    channels, rows, _ = partial_ref.shape
    part = whole.shape[1]
    for slot in range(4):
        at = 2 * (slot ^ spot)
        whole[at + core] = refs[slot][0:part]
        whole[at + 1 - core] = refs[4 + slot][0:part]
    split, blocks = spatial_ref.shape[0], channels // 16
    copies = [
        pltpu.make_async_copy(whole.at[0:split], spatial_ref, sems.at[blocks]),
        pltpu.make_async_copy(whole.at[split:], temporal_ref, sems.at[blocks + 1]),
    ]
    for copy in copies:
        copy.start()
    weight = jnp.where(core == 0, weight_ref[0].astype(F32), weight_ref[2].astype(F32)).astype(BF16)
    each = TILE // LANES
    for n in range(rows // each):
        mixed = jnp.dot(weight, outside_ref[:, span(n * each, each)], preferred_element_type=F32)
        for i in range(each):
            flat[n * each + i] = mixed[:, span(i, 1)]
    for i in range(blocks):
        at = slice(16 * i, 16 * i + 16)
        staged[at] = (partial_ref[at] + turn(flat[:, at, :])).astype(BF16)
        copies.append(pltpu.make_async_copy(staged.at[at], out_ref.at[at], sems.at[i]))
        copies[-1].start()
    for copy in copies:
        copy.wait()


def final_kernel(own_ref, one_ref, two_ref, three_ref, scaled_ref, plane_ref, columns_ref, raw_ref, out_ref, flat, staged, sems):
    channels, rows, _ = raw_ref.shape
    count = (channels // GROUPS) * rows * LANES * 8
    at = own_ref.shape[0] - 8
    totals = (own_ref[at:, :] + one_ref[at:, :]) + (two_ref[at:, :] + three_ref[at:, :])
    totals = group_sum(totals) / count
    turned = jnp.concatenate([totals, jnp.zeros((LANES - 8, LANES), F32)], axis=0).T
    wide = lambda v, at: jnp.broadcast_to(v[:, at : at + 1], (channels, LANES))
    mean_grad, second = wide(turned, 0), wide(turned, 1)
    columns = columns_ref[...]
    center, inverse = wide(columns, 0), wide(columns, 1)

    def step(r, carry):
        normed = (plane_ref[:, row_at(r)].astype(F32) - center) * inverse
        flat[r] = inverse * (scaled_ref[:, row_at(r)] - mean_grad - normed * second)
        return carry

    lax.fori_loop(0, rows, step, 0, unroll=2)
    copies = []
    for i in range(channels // 16):
        at = slice(16 * i, 16 * i + 16)
        staged[at] = (raw_ref[at].astype(F32) + turn(flat[:, at, :])).astype(BF16)
        copies.append(pltpu.make_async_copy(staged.at[at], out_ref.at[at], sems.at[i]))
        copies[-1].start()
    for copy in copies:
        copy.wait()


def body(inputs, cotangent, spatial_weight, temporal_weight, norm_gain, norm_shift, spatial_bias):
    frames = lax.axis_size("frame")
    peers = lax.axis_size("chan")
    core = lax.axis_index("frame") % 2
    me = lax.axis_index("chan")
    channels, rows, cols = inputs.shape[1:]
    pixels = rows * cols
    plane, half = (channels, pixels), (channels, pixels // 2)
    tied = lax.optimization_barrier
    at = lax.axis_index("frame")
    place = jnp.stack([me, core, me // 2, (at // 2 % 2) ^ core]).astype(jnp.int32)
    table = jnp.concatenate([v[None] for v in (norm_gain, norm_shift, spatial_bias)])
    place, table = tied((place, table))
    raw_in, raw_grad = inputs[0], cotangent[0]
    cross = lambda v: lax.ppermute(v, "frame", neighbour(frames))
    mate = lambda v: lax.ppermute(v, "frame", partner(1, frames))

    def meet(v, frame_bits, chan_bits):
        return lax.ppermute(v, ("frame", "chan"), both(frame_bits, chan_bits, frames, peers))

    def total(v, steps):
        got = [v] + [meet(v, *step) for step in steps]
        return got[0] + got[1] if len(got) == 2 else (got[0] + got[1]) + (got[2] + got[3])

    turned, payload = call(
        sums_kernel, [(plane, BF16), ((peers, 8 + rows, channels), F32)], [place, raw_in], cost=(0, 2 * MIB), limit=8
    )
    payload, later_grad = tied((payload, raw_grad))
    received = lax.all_to_all(payload, "chan", 0, 0, tiled=True)
    early_grad, late_grad = call(turn_kernel, [(half, BF16)] * 2, [later_grad], cost=(0, 1000), limit=8)
    crossed = [cross(early_grad)]
    received, early_grad, late_grad = tied((received, early_grad, late_grad))
    grads = [early_grad, late_grad]
    inside_grad = lax.ppermute(late_grad, "frame", crossing(frames, True))
    mates = [mate(v) for v in grads]

    padded = (3 * channels, pixels + 2 * cols)
    act, hidden, slope, columns = call(
        forward_kernel,
        [(padded, BF16), (plane, BF16), (plane, F32), ((channels, LANES), F32)],
        [place, turned, received, table, spatial_weight],
        cost=(1000, MIB),
        limit=16,
    )
    slope, late_grad = tied((slope, grads[1]))
    outside_grad = lax.ppermute(late_grad, "frame", crossing(frames, False))
    early_shape, late_shape = (3 * channels, channels), (3 * channels, 3 * channels)
    shifted = pltpu.VMEM((channels, pixels // 2 + 4 * cols), BF16)
    pre_early, *sums = call(
        functools.partial(backward_kernel, False),
        [(half, BF16), (early_shape, F32), (late_shape, F32), ((LANES, channels), F32)],
        [place, act, hidden, slope, grads[0], mates[0], crossed[0], temporal_weight],
        [shifted],
        cost=(1000, MIB),
        limit=20,
    )
    part = 12 * channels // 8
    slots = ((4, part, channels), F32)
    pre_late, keep, send, edges = call(
        functools.partial(backward_kernel, True),
        [(half, BF16), slots, slots, ((2 * rows, channels), F32)],
        [place, act, hidden, slope, grads[1], mates[1], outside_grad, inside_grad, temporal_weight, *sums],
        [pltpu.VMEM(early_shape, F32), pltpu.VMEM(late_shape, F32), shifted],
        cost=(1000, MIB),
        limit=20,
    )
    near = meet(edges, 0, 1)
    terms = keep + mate(send)
    terms, near, hidden = tied((terms, near, hidden))
    hidden_inside, hidden_mate = lax.ppermute(hidden, "frame", crossing(frames, True)), mate(hidden)
    far = near[rows:]
    one, two, three = [
        meet(jnp.concatenate([terms[b], far]) if b != 2 else terms[b], 0, 2 * b) for b in (1, 2, 3)
    ]
    piece = (terms[0] + one[:part]) + (two + three[:part])
    piece, one, three, hidden_mate = tied((piece, one, three, hidden_mate))
    scaled, sums = call(
        input_kernel,
        [(plane, F32), ((8, channels), F32)],
        [place, pre_early, pre_late, near, one, three, spatial_weight, turned, columns],
        [pltpu.VMEM(padded, BF16), pltpu.VMEM((channels, pixels + 2 * cols), F32)],
        cost=(1000, MIB),
        limit=16,
    )
    piece = total(piece, [(4, 0), (8, 0), (12, 0)])
    piece, sums = tied((piece, sums))
    piece = total(piece, [(28, 0)])
    both_x = total(jnp.concatenate([piece, sums]), [(0, 1)])
    both_x, hidden_inside = tied((both_x, hidden_inside))
    piece, sums = both_x[:part], both_x[part:]
    flat = pltpu.VMEM((rows, channels, cols), F32)
    (partial,) = call(
        partial_kernel,
        [(raw_in.shape, F32)],
        [place, hidden, hidden_mate, hidden_inside, temporal_weight, raw_in],
        [flat],
        cost=(1, 1),
        limit=16,
    )
    piece = total(piece, [(2, 1)])
    piece, hidden, partial = tied((jnp.concatenate([piece, sums]), hidden, partial))
    got = [piece] + [meet(piece, 0, 2 * b) for b in (1, 2, 3)]
    hidden_outside = lax.ppermute(hidden, "frame", crossing(frames, False))
    others = [mate(v) for v in got]
    staged, sems = pltpu.VMEM(raw_in.shape, BF16), pltpu.SemaphoreType.DMA((10,))
    (input_grad,) = call(
        final_kernel,
        [(raw_in.shape, BF16)],
        [*got, scaled, turned, columns, raw_grad],
        [flat, staged, sems],
        cost=(1000, MIB),
        limit=16,
        place=pl.ANY,
    )
    hidden_outside, input_grad = tied((hidden_outside, input_grad))
    spatial_grad, temporal_grad, output = call(
        close_kernel,
        [((6, part, channels), F32), ((2, part, channels), F32), (raw_in.shape, BF16)],
        [place, *got, *others, partial, hidden_outside, temporal_weight],
        [pltpu.VMEM((8, part, channels), F32), flat, staged, sems],
        cost=(1000, MIB),
        limit=16,
        place=pl.ANY,
    )
    square = (-1, channels, channels)
    return (output[None], input_grad[None], spatial_grad.reshape(square), temporal_grad.reshape(square))


def solution(mesh):
    banded = P("frame", None, None, "chan")
    return jax.shard_map(
        body,
        mesh=mesh,
        in_specs=(banded, banded, P(), P(), P(), P(), P()),
        out_specs=(banded, banded, P(), P()),
        check_vma=False,
    )
```

```python
import functools

import jax
import jax.numpy as jnp
from jax import lax
from jax.experimental import pallas as pl
from jax.experimental.pallas import tpu as pltpu
from jax.sharding import PartitionSpec as P

GROUPS = 32
LANES = 128
TILE = 1024
MIB = 1024 * 1024
CONTRACT_LAST = (((1,), (1,)), ((), ()))
F32, BF16 = jnp.float32, jnp.bfloat16


def partner(bits, frames):
    return [(f, f ^ bits) for f in range(frames)]


def both(frame_bits, chan_bits, frames, peers):
    return [(f * peers + c, (f ^ frame_bits) * peers + (c ^ chan_bits)) for f in range(frames) for c in range(peers)]


def crossing(frames, inside):
    return [(f, t) for f, t in neighbour(frames) if (f // 4 == t // 4) == inside]


def neighbour(frames):
    pairs = []
    for f in range(frames):
        target = f + 1 if f % 2 else f - 1
        if 0 <= target < frames:
            pairs.append((f, target))
    return pairs


def call(kernel, outs, ins, scratch=(), cost=(0, 0), limit=24, place=pltpu.VMEM):
    smem = pl.BlockSpec(memory_space=pltpu.SMEM)
    vmem = pl.BlockSpec(memory_space=pltpu.VMEM)
    is_place = lambda v: v.dtype == jnp.int32
    flops, moved = cost
    return pl.pallas_call(
        kernel,
        out_shape=[jax.ShapeDtypeStruct(s, d) for s, d in outs],
        in_specs=[smem if is_place(v) else vmem for v in ins],
        out_specs=[pl.BlockSpec(memory_space=place)] * len(outs),
        scratch_shapes=list(scratch),
        cost_estimate=pl.CostEstimate(flops=flops, bytes_accessed=moved, transcendentals=0),
        compiler_params=pltpu.CompilerParams(vmem_limit_bytes=limit * MIB),
    )(*ins)


def lane_index(shape=(LANES, LANES)):
    return lax.broadcasted_iota(jnp.int32, shape, len(shape) - 1)


def row_at(r):
    return pl.ds(pl.multiple_of(r * LANES, LANES), LANES)


def span(row, rows):
    return slice(row * LANES, (row + rows) * LANES)


def side(parts):
    return jnp.concatenate(parts, axis=1)


def tile_at(n, extra=0):
    return pl.ds(pl.multiple_of(n * TILE, LANES) + extra, TILE)


def group_sum(v):
    lane = lax.broadcasted_iota(jnp.int32, v.shape, 1)
    for step in (1, 2):
        up, down = pltpu.roll(v, LANES - step, 1), pltpu.roll(v, step, 1)
        v = v + jnp.where((lane // step) % 2 == 0, up, down)
    return v


def sigmoid(v):
    return 1.0 / (1.0 + jnp.exp(-v))


def selector(n, rows):
    pixel = lax.broadcasted_iota(jnp.int32, (LANES, TILE), 1) + n * TILE
    at = lax.broadcasted_iota(jnp.int32, (LANES, TILE), 0)
    low = (at < rows) & (pixel == at * LANES)
    high = (at >= 64) & (pixel == (at - 64) * LANES + (LANES - 1))
    return jnp.where(low | high | (at == 32), 1.0, 0.0).astype(BF16)


def turn(raw):
    return jnp.swapaxes(raw, 0, 1)


def store_shifts(ref, row, halo, r, lane, order, offset=1):
    row = row.astype(BF16)
    left = jnp.where(lane == 0, pltpu.roll(halo, LANES - 32 - r, 1), pltpu.roll(row, 1, 1))
    right = jnp.where(lane == LANES - 1, pltpu.roll(halo, 63 - r, 1), pltpu.roll(row, LANES - 1, 1))
    shifts = (left, row, right)
    for slot, which in enumerate(order):
        ref[slot * LANES : (slot + 1) * LANES, row_at(r + offset)] = shifts[which].astype(BF16)


def turn_kernel(raw_ref, low_ref, high_ref):
    channels, rows, _ = raw_ref.shape
    for c in range(0, channels, 16):
        block = turn(raw_ref[c : c + 16])
        for r in range(rows):
            ref, at = (low_ref, r) if r < rows // 2 else (high_ref, r - rows // 2)
            ref[c : c + 16, at * LANES : (at + 1) * LANES] = block[r]


def sums_kernel(me_ref, raw_ref, out_ref, payload_ref):
    channels, rows, _ = raw_ref.shape
    me = me_ref[0]
    for c in range(0, channels, 16):
        block = turn(raw_ref[c : c + 16])
        for r in range(rows):
            out_ref[c : c + 16, r * LANES : (r + 1) * LANES] = block[r]
    packed = jnp.zeros((LANES, channels), F32)
    for n in range(rows * LANES // TILE):
        packed += lax.dot_general(selector(n, rows), out_ref[:, n * TILE : (n + 1) * TILE], CONTRACT_LAST, preferred_element_type=F32)
    mean = packed[32:33] / (rows * LANES)
    mean_all = jnp.broadcast_to(mean, (LANES, channels)).T

    def square(r, acc):
        off = out_ref[:, row_at(r)].astype(F32) - mean_all
        return acc + off * off

    squares = lax.fori_loop(0, rows, square, jnp.zeros((channels, LANES), F32), unroll=4)
    squares = jnp.sum(squares.T, axis=0, keepdims=True)
    head = jnp.concatenate([mean, squares, jnp.zeros((6, channels), F32)], axis=0)
    for peer in range(payload_ref.shape[0]):
        payload_ref[peer, 0:8, :] = head
        payload_ref[peer, 8 : 8 + rows, :] = jnp.where(peer < me, packed[0:rows], packed[64 : 64 + rows])


def forward_kernel(me_ref, plane_ref, received_ref, table_ref, weight_ref, act_ref, hidden_ref, slope_ref, columns_ref):
    channels, pixels = plane_ref.shape
    rows = pixels // LANES
    peers = received_ref.shape[0]
    me = me_ref[0]
    lane = lane_index()
    count = (channels // GROUPS) * pixels * peers
    means, squares = received_ref[:, 0, :], received_ref[:, 1, :]
    center = group_sum(jnp.sum(means, axis=0, keepdims=True)) * (GROUPS / (channels * peers))
    off = means - center
    spread = group_sum(jnp.sum(squares + pixels * (off * off), axis=0, keepdims=True)) / count
    inverse = lax.rsqrt(spread + 1e-05)
    low = received_ref[jnp.maximum(me - 1, 0), 8 : 8 + rows, :]
    high = received_ref[jnp.minimum(me + 1, peers - 1), 8 : 8 + rows, :]
    head = jnp.concatenate([center, inverse, table_ref[...], jnp.zeros((3, LANES), F32)], axis=0)
    gap = jnp.zeros((24, LANES), F32)
    columns = jnp.concatenate([head, gap, low, high, jnp.zeros((32, LANES), F32)], axis=0).T
    columns_ref[...] = columns
    wide = lambda at: jnp.broadcast_to(columns[:, at : at + 1], (channels, LANES))
    center_w, inverse_w, gain_w, shift_w, bias_w = [wide(at) for at in range(5)]

    def activate(v):
        v = (v - center_w) * inverse_w * gain_w + shift_w
        return v * sigmoid(v)

    inside = ((lane < 64) & (me > 0)) | ((lane >= 64) & (me < peers - 1))
    halo = jnp.where(inside, activate(columns), 0.0).astype(BF16)
    nothing = jnp.zeros((3 * channels, LANES), BF16)
    act_ref[:, 0:LANES] = nothing
    act_ref[:, (rows + 1) * LANES : (rows + 2) * LANES] = nothing

    def shape_row(r, carry):
        row = activate(plane_ref[:, row_at(r)].astype(F32))
        store_shifts(act_ref, row, halo, r, lane, (0, 1, 2))
        return carry

    lax.fori_loop(0, rows, shape_row, 0, unroll=8)
    weights = side([weight_ref[t] for t in range(9)])
    each = TILE // LANES
    bias = jnp.broadcast_to(bias_w[:, 0:1], (channels, TILE))
    for n in range(rows // each):
        window = jnp.concatenate([act_ref[:, span(n * each + dy, each)] for dy in range(3)], axis=0)
        value = jnp.dot(weights, window, preferred_element_type=F32) + bias
        logistic = sigmoid(value)
        hidden_ref[:, span(n * each, each)] = (value * logistic).astype(BF16)
        slope_ref[:, span(n * each, each)] = logistic * (1.0 + value * (1.0 - logistic))


def backward_kernel(last, me_ref, act_ref, hidden_ref, slope_ref, grad_ref, mate_ref, cross_ref, *rest):
    if last:
        inside_ref, weight_ref, early_in, late_in, packed_in, *rest = rest
        inside = me_ref[3] == 1
        pre_ref, keep_ref, send_ref, edges_ref, early, late, shifted = rest
    else:
        weight_ref, pre_ref, early, late, packed_ref, shifted = rest
    channels, pixels = grad_ref.shape
    rows = 2 * pixels // LANES
    core, spot = me_ref[1], me_ref[2]
    turned = [weight_ref[k].astype(F32).T for k in range(3)]
    even = core == 0
    ahead = jnp.where(even, turned[0], turned[2])
    behind = jnp.where(even, turned[2], turned[0])
    weights = jnp.concatenate([turned[1], ahead, behind], axis=1).astype(BF16)
    own_rows = rows // 2
    start = own_rows if last else 0
    blank = jnp.zeros((channels, 2 * LANES), BF16)
    shifted[:, span(0, 2)] = blank
    shifted[:, span(own_rows + 2, 2)] = blank
    each = TILE // LANES
    fresh = jnp.zeros((3 * channels, channels), F32)
    packed = jnp.zeros((LANES, channels), F32)
    for n in range(own_rows // each):
        at, whole = span(n * each, each), span(n * each + start, each)
        across = cross_ref[:, at]
        if last:
            across = jnp.where(inside, inside_ref[:, at], across)
        grads = jnp.concatenate([grad_ref[:, at], mate_ref[:, at], across], axis=0)
        back = jnp.dot(weights, grads, preferred_element_type=F32)
        pre = (back * slope_ref[:, whole]).astype(BF16)
        pre_ref[:, at] = pre
        shifted[:, span(n * each + 2, each)] = pre
        fresh += lax.dot_general(grads, hidden_ref[:, whole], CONTRACT_LAST, preferred_element_type=F32)
        packed += lax.dot_general(selector(n + start // each, rows), pre, CONTRACT_LAST, preferred_element_type=F32)
    lhs = jnp.concatenate([shifted[:, span(2 - dy, own_rows + 2)] for dy in range(3)], axis=0)
    rhs = act_ref[:, span(start, own_rows + 2)]
    latest = lax.dot_general(lhs, rhs, CONTRACT_LAST, preferred_element_type=F32)
    early[...] = fresh + early_in[...] if last else fresh
    late[...] = latest + late_in[...] if last else latest
    packed = packed + packed_in[...] if last else packed
    if not last:
        packed_ref[...] = packed
        return
    low, high = packed[0:rows], packed[64 : 64 + rows]
    left = me_ref[0] % 2 == 0
    edges_ref[0:rows, :] = jnp.where(left, high, low)
    edges_ref[rows:, :] = jnp.where(left, low, high)
    own, mate, cross = [early[i * channels : (i + 1) * channels, :] for i in range(3)]
    blocks = [late[t // 3 * channels : (t // 3 + 1) * channels, span(t % 3, 1)] for t in range(9)]
    blocks += [jnp.where(even, mate, cross), own, jnp.where(even, cross, mate)]
    part = keep_ref.shape[1]

    def rows_at(at):
        return blocks[at // channels][at % channels : at % channels + 64]

    for y in range(4):
        slot = y ^ spot
        for v in range(0, part, 64):
            one, two = rows_at(2 * y * part + v), rows_at((2 * y + 1) * part + v)
            keep_ref[slot, v : v + 64, :] = jnp.where(even, one, two)
            send_ref[slot, v : v + 64, :] = jnp.where(even, two, one)


def input_kernel(me_ref, early_ref, late_ref, near_ref, one_ref, three_ref, *refs):
    weight_ref, plane_ref, columns_ref, scaled_ref, sums_ref, padded, total = refs
    channels, pixels = plane_ref.shape
    rows = pixels // LANES
    lane = lane_index()
    blank = jnp.zeros((32, LANES), F32)
    me = me_ref[0]
    left = me % 2 == 0
    near = near_ref[0:rows, :]
    at = one_ref.shape[0] - rows
    far = jnp.where((me // 2 % 2 == 0) != left, one_ref[at:, :], three_ref[at:, :])
    far = jnp.where((me > 0) & (me < 7), far, 0.0)
    low, high = jnp.where(left, far, near), jnp.where(left, near, far)
    halo = jnp.concatenate([blank, low, high, blank], axis=0).T.astype(BF16)
    for first, ref in ((0, early_ref), (rows // 2, late_ref)):

        def shift_row(r, carry, ref=ref, first=first):
            store_shifts(padded, ref[:, row_at(r)], halo, r + first, lane, (2, 1, 0))
            return carry

        lax.fori_loop(0, rows // 2, shift_row, 0, unroll=8)
    flipped = lambda t: weight_ref[t].astype(F32).T.astype(BF16)
    weights = side([flipped(3 * dy + dx) for dy in (2, 1, 0) for dx in range(3)])
    each = TILE // LANES
    padded[:, span(0, 1)] = jnp.zeros((3 * channels, LANES), BF16)
    padded[:, span(rows + 1, 1)] = jnp.zeros((3 * channels, LANES), BF16)
    for n in range(rows // each):
        window = jnp.concatenate([padded[:, span(n * each + dy, each)] for dy in range(3)], axis=0)
        total[:, span(n * each + 1, each)] = jnp.dot(weights, window, preferred_element_type=F32)
    columns = columns_ref[...]
    wide = lambda at: jnp.broadcast_to(columns[:, at : at + 1], (channels, LANES))
    center, inverse, gain, shift = [wide(at) for at in range(4)]

    def step(r, carry):
        plain, crossed = carry
        normed = (plane_ref[:, row_at(r)].astype(F32) - center) * inverse
        shaped = normed * gain + shift
        logistic = sigmoid(shaped)
        scaled = total[:, row_at(r + 1)] * (logistic * (1.0 + shaped * (1.0 - logistic))) * gain
        scaled_ref[:, row_at(r)] = scaled
        return plain + scaled, crossed + scaled * normed

    zero = jnp.zeros((channels, LANES), F32)
    plain, crossed = lax.fori_loop(0, rows, step, (zero, zero), unroll=4)
    plain, crossed = [jnp.sum(v, axis=1, keepdims=True) for v in (plain, crossed)]
    sums_ref[...] = jnp.where(lane == 0, plain, jnp.where(lane == 1, crossed, 0.0)).T[0:8]


def partial_kernel(me_ref, hidden_ref, mate_ref, inside_ref, weight_ref, raw_ref, out_ref, flat):
    channels, rows, _ = raw_ref.shape
    even = me_ref[1] == 0
    pick = lambda a, b: jnp.where(even, weight_ref[a].astype(F32), weight_ref[b].astype(F32)).astype(BF16)
    weights = jnp.concatenate([weight_ref[1], pick(2, 0), pick(0, 2)], axis=1)
    each = TILE // LANES
    for n in range(rows // each):
        at = span(n * each, each)
        frames = jnp.concatenate([ref[:, at] for ref in (hidden_ref, mate_ref, inside_ref)], axis=0)
        mixed = jnp.dot(weights, frames, preferred_element_type=F32)
        for i in range(each):
            flat[n * each + i] = mixed[:, span(i, 1)]
    for c in range(0, channels, 16):
        out_ref[c : c + 16] = raw_ref[c : c + 16].astype(F32) + turn(flat[:, c : c + 16, :])


def close_kernel(me_ref, *refs):
    partial_ref, outside_ref, weight_ref, spatial_ref, temporal_ref, out_ref, whole, flat, staged, sems = refs[8:]
    core, spot = me_ref[1], me_ref[2]
    channels, rows, _ = partial_ref.shape
    part = whole.shape[1]
    for slot in range(4):
        at = 2 * (slot ^ spot)
        whole[at + core] = refs[slot][0:part]
        whole[at + 1 - core] = refs[4 + slot][0:part]
    split, blocks = spatial_ref.shape[0], channels // 16
    copies = [
        pltpu.make_async_copy(whole.at[0:split], spatial_ref, sems.at[blocks]),
        pltpu.make_async_copy(whole.at[split:], temporal_ref, sems.at[blocks + 1]),
    ]
    for copy in copies:
        copy.start()
    weight = jnp.where(core == 0, weight_ref[0].astype(F32), weight_ref[2].astype(F32)).astype(BF16)
    each = TILE // LANES
    for n in range(rows // each):
        mixed = jnp.dot(weight, outside_ref[:, span(n * each, each)], preferred_element_type=F32)
        for i in range(each):
            flat[n * each + i] = mixed[:, span(i, 1)]
    for i in range(blocks):
        at = slice(16 * i, 16 * i + 16)
        staged[at] = (partial_ref[at] + turn(flat[:, at, :])).astype(BF16)
        copies.append(pltpu.make_async_copy(staged.at[at], out_ref.at[at], sems.at[i]))
        copies[-1].start()
    for copy in copies:
        copy.wait()


def final_kernel(own_ref, one_ref, two_ref, three_ref, scaled_ref, plane_ref, columns_ref, raw_ref, out_ref, flat, staged, sems):
    channels, rows, _ = raw_ref.shape
    count = (channels // GROUPS) * rows * LANES * 8
    at = own_ref.shape[0] - 8
    totals = (own_ref[at:, :] + one_ref[at:, :]) + (two_ref[at:, :] + three_ref[at:, :])
    totals = group_sum(totals) / count
    turned = jnp.concatenate([totals, jnp.zeros((LANES - 8, LANES), F32)], axis=0).T
    wide = lambda v, at: jnp.broadcast_to(v[:, at : at + 1], (channels, LANES))
    mean_grad, second = wide(turned, 0), wide(turned, 1)
    columns = columns_ref[...]
    center, inverse = wide(columns, 0), wide(columns, 1)

    def step(r, carry):
        normed = (plane_ref[:, row_at(r)].astype(F32) - center) * inverse
        flat[r] = inverse * (scaled_ref[:, row_at(r)] - mean_grad - normed * second)
        return carry

    lax.fori_loop(0, rows, step, 0, unroll=2)
    copies = []
    for i in range(channels // 16):
        at = slice(16 * i, 16 * i + 16)
        staged[at] = (raw_ref[at].astype(F32) + turn(flat[:, at, :])).astype(BF16)
        copies.append(pltpu.make_async_copy(staged.at[at], out_ref.at[at], sems.at[i]))
        copies[-1].start()
    for copy in copies:
        copy.wait()


def body(inputs, cotangent, spatial_weight, temporal_weight, norm_gain, norm_shift, spatial_bias):
    frames = lax.axis_size("frame")
    peers = lax.axis_size("chan")
    core = lax.axis_index("frame") % 2
    me = lax.axis_index("chan")
    channels, rows, cols = inputs.shape[1:]
    pixels = rows * cols
    plane, half = (channels, pixels), (channels, pixels // 2)
    tied = lax.optimization_barrier
    at = lax.axis_index("frame")
    place = jnp.stack([me, core, me // 2, (at // 2 % 2) ^ core]).astype(jnp.int32)
    table = jnp.concatenate([v[None] for v in (norm_gain, norm_shift, spatial_bias)])
    place, table = tied((place, table))
    raw_in, raw_grad = inputs[0], cotangent[0]
    cross = lambda v: lax.ppermute(v, "frame", neighbour(frames))
    mate = lambda v: lax.ppermute(v, "frame", partner(1, frames))

    def meet(v, frame_bits, chan_bits):
        return lax.ppermute(v, ("frame", "chan"), both(frame_bits, chan_bits, frames, peers))

    def total(v, steps):
        got = [v] + [meet(v, *step) for step in steps]
        return got[0] + got[1] if len(got) == 2 else (got[0] + got[1]) + (got[2] + got[3])

    turned, payload = call(
        sums_kernel, [(plane, BF16), ((peers, 8 + rows, channels), F32)], [place, raw_in], cost=(0, 2 * MIB), limit=8
    )
    payload, later_grad = tied((payload, raw_grad))
    received = lax.all_to_all(payload, "chan", 0, 0, tiled=True)
    early_grad, late_grad = call(turn_kernel, [(half, BF16)] * 2, [later_grad], cost=(0, 1000), limit=8)
    crossed = [cross(early_grad)]
    received, early_grad, late_grad = tied((received, early_grad, late_grad))
    grads = [early_grad, late_grad]
    inside_grad = lax.ppermute(late_grad, "frame", crossing(frames, True))
    mates = [mate(v) for v in grads]

    padded = (3 * channels, pixels + 2 * cols)
    act, hidden, slope, columns = call(
        forward_kernel,
        [(padded, BF16), (plane, BF16), (plane, F32), ((channels, LANES), F32)],
        [place, turned, received, table, spatial_weight],
        cost=(1000, MIB),
        limit=16,
    )
    slope, late_grad = tied((slope, grads[1]))
    outside_grad = lax.ppermute(late_grad, "frame", crossing(frames, False))
    early_shape, late_shape = (3 * channels, channels), (3 * channels, 3 * channels)
    shifted = pltpu.VMEM((channels, pixels // 2 + 4 * cols), BF16)
    pre_early, *sums = call(
        functools.partial(backward_kernel, False),
        [(half, BF16), (early_shape, F32), (late_shape, F32), ((LANES, channels), F32)],
        [place, act, hidden, slope, grads[0], mates[0], crossed[0], temporal_weight],
        [shifted],
        cost=(1000, MIB),
        limit=20,
    )
    part = 12 * channels // 8
    slots = ((4, part, channels), F32)
    pre_late, keep, send, edges = call(
        functools.partial(backward_kernel, True),
        [(half, BF16), slots, slots, ((2 * rows, channels), F32)],
        [place, act, hidden, slope, grads[1], mates[1], outside_grad, inside_grad, temporal_weight, *sums],
        [pltpu.VMEM(early_shape, F32), pltpu.VMEM(late_shape, F32), shifted],
        cost=(1000, MIB),
        limit=20,
    )
    near = meet(edges, 0, 1)
    terms = keep + mate(send)
    terms, near, hidden = tied((terms, near, hidden))
    hidden_inside, hidden_mate = lax.ppermute(hidden, "frame", crossing(frames, True)), mate(hidden)
    far = near[rows:]
    one, two, three = [
        meet(jnp.concatenate([terms[b], far]) if b != 2 else terms[b], 0, 2 * b) for b in (1, 2, 3)
    ]
    piece = (terms[0] + one[:part]) + (two + three[:part])
    piece, one, three, hidden_mate = tied((piece, one, three, hidden_mate))
    scaled, sums = call(
        input_kernel,
        [(plane, F32), ((8, channels), F32)],
        [place, pre_early, pre_late, near, one, three, spatial_weight, turned, columns],
        [pltpu.VMEM(padded, BF16), pltpu.VMEM((channels, pixels + 2 * cols), F32)],
        cost=(1000, MIB),
        limit=16,
    )
    piece = total(piece, [(4, 0), (8, 0), (12, 0)])
    piece, sums = tied((piece, sums))
    piece = total(piece, [(28, 0)])
    both_x = total(jnp.concatenate([piece, sums]), [(0, 1)])
    both_x, hidden_inside = tied((both_x, hidden_inside))
    piece, sums = both_x[:part], both_x[part:]
    flat = pltpu.VMEM((rows, channels, cols), F32)
    (partial,) = call(
        partial_kernel,
        [(raw_in.shape, F32)],
        [place, hidden, hidden_mate, hidden_inside, temporal_weight, raw_in],
        [flat],
        cost=(1, 1),
        limit=16,
    )
    far_sum, sent, partial = tied((meet(piece, 2, 1), hidden, partial))
    hidden_outside = lax.ppermute(sent, "frame", crossing(frames, False))
    piece = jnp.concatenate([piece + far_sum, sums])
    got = [piece] + [meet(piece, 0, 2 * b) for b in (1, 2, 3)]
    others = [mate(v) for v in got]
    staged, sems = pltpu.VMEM(raw_in.shape, BF16), pltpu.SemaphoreType.DMA((10,))
    (input_grad,) = call(
        final_kernel,
        [(raw_in.shape, BF16)],
        [*got, scaled, turned, columns, raw_grad],
        [flat, staged, sems],
        cost=(1000, MIB),
        limit=16,
        place=pl.ANY,
    )
    hidden_outside, input_grad = tied((hidden_outside, input_grad))
    spatial_grad, temporal_grad, output = call(
        close_kernel,
        [((6, part, channels), F32), ((2, part, channels), F32), (raw_in.shape, BF16)],
        [place, *got, *others, partial, hidden_outside, temporal_weight],
        [pltpu.VMEM((8, part, channels), F32), flat, staged, sems],
        cost=(1000, MIB),
        limit=16,
        place=pl.ANY,
    )
    square = (-1, channels, channels)
    return (output[None], input_grad[None], spatial_grad.reshape(square), temporal_grad.reshape(square))


def solution(mesh):
    banded = P("frame", None, None, "chan")
    return jax.shard_map(
        body,
        mesh=mesh,
        in_specs=(banded, banded, P(), P(), P(), P(), P()),
        out_specs=(banded, banded, P(), P()),
        check_vma=False,
    )
```
